32 devices in a mesh: groups: 2 (over y), row: 16 (over z, x, core).
Axes of the slice: x: 2, y: 2, z: 4, core: 2. Of those that a mesh axis runs over, the one named last changes fastest.
Arguments:
- attn_out: bfloat16 [256, 8192], P('groups', 'row'), parts along dimension 0, may hold values from -6 to 6
- residual_in: bfloat16 [16, 128, 1024], P('row', 'groups'), parts along dimension 1, may hold values from -32 to 32
- out_weight: bfloat16 [16, 4096, 1024], P('row'), may hold values from -0.0625 to 0.0625
- norm_gain: float32 [8192], replicated, may hold values from 0.1 to 1.9
- gate_weight: bfloat16 [16, 1024, 7168], P('row'), may hold values from -0.0625 to 0.0625
- up_weight: bfloat16 [16, 1024, 7168], P('row'), may hold values from -0.0625 to 0.0625
- down_weight: bfloat16 [16, 7168, 1024], P('row'), may hold values from -0.046875 to 0.046875
Outputs:
- layer_out: bfloat16 [256, 16, 512], P('groups', 'row'), parts along dimension 0
The draws below stay inside these ranges and needn't reach their ends.
There are 2 independent parts, one for each index of `groups`. The reference program is written for one: setup_inputs(seed, part) draws one part's arguments, and reference() takes and returns one part's arrays. A program takes and returns all parts, laid end to end along the dimension named above; an argument that names none is the same for every part. Nothing has to cross between parts.
All inputs are finite; a program needn't handle non-finite values.
Results may differ from the reference program's by a relative error of at most 0.0055.
Values may be sent and summed in bfloat16 or wider, within the bound.
A program may use at most 128 MiB of HBM per device.

```python
import math
import jax
import jax.numpy as jnp
from jax import lax

D = 8192
FF = 14336
TOKENS = 128
COLG = 8
ROWG = 2
N_ROW = 16


def draw_residual_in(key, part):
    key_noise, key_rows, key_cols = jax.random.split(key, 3)
    tile_shape = (N_ROW, TOKENS // ROWG, D // COLG)
    noise = jnp.clip(jax.random.normal(key_noise, tile_shape, jnp.float32), -3.5, 3.5)
    row_scale = 0.3 * jnp.exp(jax.random.uniform(key_rows, (N_ROW, TOKENS // ROWG, 1), jnp.float32, 0.0, math.log(10.0)))
    col_scale = jnp.exp(jax.random.uniform(key_cols, (N_ROW, 1, D // COLG), jnp.float32, math.log(0.3), 0.0))
    tile_column = (jnp.arange(N_ROW) % COLG).astype(jnp.float32)
    rising = jnp.exp(math.log(3.0) * tile_column / (COLG - 1)).reshape(N_ROW, 1, 1)
    return (noise * row_scale * col_scale * rising).astype(jnp.bfloat16)


def with_spikes(array, rng, source, target, shards_of, factor):
    owner, partner = [(jnp.arange(array.shape[position]) // (array.shape[position] // shards_of)).reshape([-1 if axis == position else 1 for axis in range(array.ndim)]) for position in (source, target)]
    chosen = jax.random.permutation(rng, shards_of)[partner]
    strong = (owner == chosen) | (owner == (partner + shards_of // 2) % shards_of)
    return jnp.where(strong, factor * array, array)


def block_levels(own_key, dims, pieces, low, top_value):
    level, own = 1.0, jax.random.fold_in(own_key, 6)
    for dim, shards_of in pieces:
        steps = jnp.exp(jax.random.uniform(jax.random.fold_in(own, dim), (shards_of,), jnp.float32, low / len(pieces), top_value / len(pieces)))
        level = level * jnp.repeat(steps, dims[dim] // shards_of).reshape([-1 if axis == dim else 1 for axis in range(len(dims))])
    return level


def scatter_about(rng, extent, scale, most, pieces=(), kind=jnp.bfloat16):
    factor_of = block_levels(rng, extent, pieces, -0.22, 0.18) if pieces else 1.0
    values = jax.random.normal(rng, extent, jnp.float32) * scale * factor_of
    return jnp.minimum(jnp.maximum(values, -most), most).astype(kind)


def gaussian_with(own_key, extent, width, reach, cuts, heavy, dtype=jnp.bfloat16):
    array = width * jax.random.normal(own_key, extent, jnp.float32)
    if cuts:
        array = array * block_levels(own_key, extent, cuts, -0.22, 0.18)
    return jnp.clip(with_spikes(array, jax.random.fold_in(own_key, 3), *heavy), -reach, reach).astype(dtype)


def setup_inputs(seed: int = 0, part: int = 0) -> dict:
    key_of = jax.random.split(jax.random.key(seed), 8)
    part_splits = jax.random.split(jax.random.fold_in(key_of[7], part), 8)
    return {
        "attn_out": gaussian_with(part_splits[0], (TOKENS, D), 1.0, 6.0, ((1, 16),), (1, 0, 16, 2.0)),
        "residual_in": draw_residual_in(jax.random.fold_in(jax.random.fold_in(key_of[7], part), 71), part),
        "out_weight": scatter_about(key_of[2], (N_ROW, D // ROWG, D // COLG), D ** -0.5, 0.0625, ((0, 16),)),
        "norm_gain": jnp.clip(1.0 + 0.18 * jax.random.normal(key_of[3], (D,), jnp.float32), 0.1, 1.9),
        "gate_weight": scatter_about(key_of[4], (N_ROW, D // COLG, FF // ROWG), D ** -0.5, 0.0625, ((0, 16),)),
        "up_weight": scatter_about(key_of[5], (N_ROW, D // COLG, FF // ROWG), D ** -0.5, 0.0625, ((0, 16),)),
        "down_weight": scatter_about(key_of[6], (N_ROW, FF // ROWG, D // COLG), FF ** -0.5, 0.046875, ((0, 16),)),
    }


def untile(tile_set, grid_rows, grid_cols):
    tile_count, block_rows, block_cols = tile_set.shape
    return tile_set.reshape(grid_rows, grid_cols, block_rows, block_cols).transpose(0, 2, 1, 3).reshape(grid_rows * block_rows, grid_cols * block_cols)

def untile_swapped(tile_set, grid_rows, grid_cols):
    tile_count, block_rows, block_cols = tile_set.shape
    return tile_set.reshape(grid_rows, grid_cols, block_rows, block_cols).transpose(1, 2, 0, 3).reshape(grid_cols * block_rows, grid_rows * block_cols)

def reference(attn_out, residual_in, out_weight, norm_gain, gate_weight, up_weight, down_weight):
    residual_whole = untile(residual_in, ROWG, COLG)
    out_whole = untile(out_weight, ROWG, COLG)
    gate_whole = untile_swapped(gate_weight, ROWG, COLG)
    up_whole = untile_swapped(up_weight, ROWG, COLG)
    down_whole = untile(down_weight, ROWG, COLG)
    projected = jnp.dot(attn_out, out_whole, preferred_element_type=jnp.float32)
    stream = (residual_whole.astype(jnp.float32) + projected).astype(jnp.bfloat16)
    widened = stream.astype(jnp.float32)
    mean_square = lax.optimization_barrier(jnp.mean(widened * widened, axis=-1, keepdims=True))
    normed = (widened * jax.lax.rsqrt(mean_square + 1e-05) * norm_gain).astype(jnp.bfloat16)
    gate_vals = jnp.dot(normed, gate_whole, preferred_element_type=jnp.float32)
    up_vals = jnp.dot(normed, up_whole, preferred_element_type=jnp.float32)
    hidden = (jax.nn.silu(gate_vals) * up_vals).astype(jnp.bfloat16)
    mlp_sum = jnp.dot(hidden, down_whole, preferred_element_type=jnp.float32)
    whole_out = (widened + mlp_sum).astype(jnp.bfloat16)
    tok_rows = whole_out.shape[0]
    piece_width = D // N_ROW
    return whole_out.reshape(tok_rows, COLG, ROWG, piece_width).transpose(0, 2, 1, 3).reshape(tok_rows, N_ROW, piece_width)
```

```python
import functools

import jax
import jax.numpy as jnp
from jax import lax
from jax.experimental import pallas as pl
from jax.experimental.pallas import tpu as pltpu
from jax.sharding import PartitionSpec as P

D = 8192
COLG = 8


def from_partner(value, axis, stride):
    mask = 2**stride
    pairs = [(source, source ^ mask) for source in range(lax.axis_size(axis))]
    return lax.ppermute(value, axis, pairs)


def gather_bits(value, dim, bit_list, device_pos, sender):
    for bit_pos in bit_list:
        incoming = sender(value, bit_pos)
        on_low = device_pos >> bit_pos & 1 == 0
        value = jnp.where(
            on_low, jnp.concatenate([value, incoming], dim), jnp.concatenate([incoming, value], dim)
        )
    return value


def reduce_bits(value, dim, bit_list, device_pos, sender):
    for bit_pos in reversed(bit_list):
        middle = value.shape[dim] // 2
        bottom = lax.slice_in_dim(value, 0, middle, axis=dim)
        top_part = lax.slice_in_dim(value, middle, 2 * middle, axis=dim)
        on_low = device_pos >> bit_pos & 1 == 0
        kept = jnp.where(on_low, bottom, top_part)
        outgoing = jnp.where(on_low, top_part, bottom)
        value = kept + sender(outgoing, bit_pos)
    return value


def sum_bits(value, bit_list, sender):
    for bit_pos in bit_list:
        value = value + sender(value, bit_pos)
    return value


def local(attn_out, residual_in, out_weight, norm_gain, gate_weight, up_weight, down_weight):
    all_bits = lax.axis_size("row").bit_length() - 1
    col_count = COLG.bit_length() - 1
    col_bits = list(range(col_count))
    row_bits = list(range(col_count, all_bits))
    device_pos = lax.axis_index("row")
    col_index = device_pos % COLG
    row_index = device_pos // COLG
    panel_in = gather_bits(
        attn_out,
        1,
        col_bits,
        device_pos,
        lambda block_piece, bit_pos: from_partner(block_piece, "row", bit_pos),
    )
    partial_proj = jnp.dot(panel_in, out_weight[0], preferred_element_type=jnp.float32)
    projected = reduce_bits(
        partial_proj,
        0,
        row_bits,
        device_pos,
        lambda block_piece, bit_pos: from_partner(block_piece, "row", bit_pos),
    )
    stream = (residual_in[0].astype(jnp.float32) + projected).astype(jnp.bfloat16)
    widened = stream.astype(jnp.float32)
    feat_cols = widened.shape[1]
    squares = jnp.sum(widened * widened, axis=-1)
    squares = sum_bits(
        squares, col_bits, lambda block_piece, bit_pos: from_partner(block_piece, "row", bit_pos)
    )
    mean_square = (squares / D)[:, None]
    gain_part = lax.dynamic_slice_in_dim(norm_gain, col_index * feat_cols, feat_cols)
    normed = (widened * lax.rsqrt(mean_square + 1e-05) * gain_part).astype(jnp.bfloat16)
    token_rows = gather_bits(
        normed,
        0,
        row_bits,
        device_pos,
        lambda block_piece, bit_pos: from_partner(block_piece, "row", bit_pos),
    )
    gate_vals = jnp.dot(token_rows, gate_weight[0], preferred_element_type=jnp.float32)
    up_vals = jnp.dot(token_rows, up_weight[0], preferred_element_type=jnp.float32)
    stacked = jnp.stack([gate_vals, up_vals])
    summed = reduce_bits(
        stacked,
        1,
        col_bits,
        device_pos,
        lambda block_piece, bit_pos: from_partner(block_piece, "row", bit_pos),
    )
    hidden = (jax.nn.silu(summed[0]) * summed[1]).astype(jnp.bfloat16)
    hidden_rows = gather_bits(
        hidden,
        0,
        col_bits,
        device_pos,
        lambda block_piece, bit_pos: from_partner(block_piece, "row", bit_pos),
    )
    partial_down = jnp.dot(hidden_rows, down_weight[0], preferred_element_type=jnp.float32)
    piece_width = feat_cols // 2 ** len(row_bits)
    stream_rows = gather_bits(
        stream,
        0,
        row_bits,
        device_pos,
        lambda block_piece, bit_pos: from_partner(block_piece, "row", bit_pos),
    )
    stream_piece = lax.dynamic_slice_in_dim(stream_rows, row_index * piece_width, piece_width, 1)
    down_piece = reduce_bits(
        partial_down,
        1,
        row_bits,
        device_pos,
        lambda block_piece, bit_pos: from_partner(block_piece, "row", bit_pos),
    )
    result = (stream_piece.astype(jnp.float32) + down_piece).astype(jnp.bfloat16)
    return result[:, None, :]


BF = jnp.bfloat16
F32 = jnp.float32
CORE, XNBR, ZNBR, OTHER = 1, 2, 4, 8
PAIRS = 4


def grid_kernel(
    attn, resid, wo, gain, wg, wu, wd, out,
    wgb, wub, wdb, panel, resb, gainb, pbuf, psend, precv, stream, xb, acc,
    sq_out, sq_in, scale, keep, send1, recv1, send2, recv2, send3, recv3, hb,
    dsend, drecv, lsem, ssem, rsem,
):
    idx = lax.axis_index("row")
    core, xpos, zpos, gr = idx % 2, idx // 2 % 2, idx // 4 % 2, idx // 8
    bits = (core, xpos, zpos, gr)
    toks, width = pbuf.shape
    blk = toks // 8
    half = toks // 2
    feat = panel.shape[2]
    wide = wgb.shape[1] // PAIRS
    sub = wide // 2
    out_w = width // 2

    def peer(mask):
        moved = idx
        for pos, bit in enumerate(bits):
            if mask >> pos & 1:
                moved = moved + (1 - 2 * bit) * 2**pos
        return moved

    def token_block(k):
        flip = lambda bit, on: 1 - bit if on else bit
        block = flip(core, k >> 2 & 1) * 4 + flip(xpos, k >> 1 & 1) * 2 + flip(zpos, k & 1)
        return pl.multiple_of(block * blk, blk)

    count = [0]
    sent = []
    local_count = [0]

    def push(src, dst, mask):
        n = count[0]
        count[0] += 1
        copy = pltpu.make_async_remote_copy(
            src_ref=src, dst_ref=dst, send_sem=ssem.at[n], recv_sem=rsem.at[n],
            device_id={"row": peer(mask)}, device_id_type=pl.DeviceIdType.MESH,
        )
        copy.start()
        sent.append(copy)
        return copy

    def fetch(src, dst):
        n = local_count[0]
        local_count[0] += 1
        copy = pltpu.make_async_copy(src, dst, lsem.at[n])
        copy.start()
        return copy

    own_load = fetch(attn, panel.at[0])
    wo_load = {}
    for d in (0, 2, 4, 1, 3, 5, 6, 7):
        first = pl.multiple_of((peer(d) - gr * 8) * feat, feat)
        wo_load[d] = fetch(wo.at[0, pl.ds(first, feat), :], wdb.at[d * feat : (d + 1) * feat])
    res_load = fetch(resid.at[0], resb)
    gain_load = fetch(gain.at[pl.ds(pl.multiple_of(idx % 8 * 8, 8), 8), :], gainb)

    barrier = pltpu.get_barrier_semaphore()
    for mask in (1, 2, 3, 4, 5, 6, 7, 8):
        pl.semaphore_signal(
            barrier, inc=1, device_id={"row": peer(mask)}, device_id_type=pl.DeviceIdType.MESH
        )
    pl.semaphore_wait(barrier, 8)

    from_x = push(attn, panel.at[XNBR], XNBR)
    from_z = push(attn, panel.at[ZNBR], ZNBR)
    from_core = push(attn, panel.at[CORE], CORE)

    def project(d):
        return jnp.dot(
            panel[d], wdb[d * feat : (d + 1) * feat, :], preferred_element_type=F32
        )

    own_load.wait()
    wo_load[0].wait()
    pbuf[...] = project(0)
    from_x.wait_recv()
    diag_z = push(panel.at[2, 0:half], panel.at[6, 0:half], ZNBR)
    core_x = push(panel.at[2], panel.at[3], CORE)
    from_z.wait_recv()
    diag_x = push(panel.at[4, half:toks], panel.at[6, half:toks], XNBR)
    core_z = push(panel.at[4], panel.at[5], CORE)
    for d in (1, 2, 4, 3, 5, 6, 7):
        wo_load[d].wait()
    gate_load, up_load = [], []
    for p in range(PAIRS):
        cols = slice(p * wide, (p + 1) * wide)
        gate_load.append(fetch(wg.at[0, :, cols], wgb.at[:, cols]))
        up_load.append(fetch(wu.at[0, :, cols], wub.at[:, cols]))
    pbuf[...] += project(2)
    pbuf[...] += project(4)
    from_core.wait_recv()
    pbuf[...] += project(1)
    diag_z.wait_recv()
    diag_x.wait_recv()
    core_d = push(panel.at[6], panel.at[7], CORE)
    pbuf[...] += project(6)
    core_x.wait_recv()
    pbuf[...] += project(3)
    core_z.wait_recv()
    pbuf[...] += project(5)
    core_d.wait_recv()
    pbuf[...] += project(7)

    res_load.wait()
    mine = pl.ds(pl.multiple_of(gr * half, half), half)
    pbuf[mine, :] += resb[...].astype(F32)
    psend[...] = pbuf[...].astype(BF)
    from_other = push(psend, precv, OTHER)
    down_load = []
    for p in range(PAIRS):
        rows = slice(p * wide, (p + 1) * wide)
        both = []
        for side, owner in ((0, gr), (1, 1 - gr)):
            first = pl.multiple_of(owner * out_w, out_w)
            both.append(
                fetch(
                    wd.at[0, rows, pl.ds(first, out_w)],
                    wdb.at[rows, side * out_w : (side + 1) * out_w],
                )
            )
        down_load.append(both)
    gain_load.wait()
    gain_row = jnp.concatenate([gainb[j : j + 1, :] for j in range(8)], axis=1)
    from_other.wait_recv()
    pbuf[...] += precv[...].astype(F32)
    for k in range(8):
        value = pbuf[pl.ds(token_block(k), blk), :]
        stream[k * blk : (k + 1) * blk, :] = value
        xb[k * blk : (k + 1) * blk, :] = (value * gain_row).astype(BF)

    sq_copies = []

    def send_squares():
        total = pbuf[...]
        total = jnp.sum(total * total, axis=1, keepdims=True)
        sq_out[...] = jnp.transpose(jnp.broadcast_to(total, (toks, toks)))[0:8, :]
        for mask in range(1, 8):
            sq_copies.append(push(sq_out, sq_in.at[mask - 1], mask))

    def make_scale():
        total = sq_out[...]
        for copy in sq_copies:
            copy.wait_recv()
        for k in range(7):
            total = total + sq_in[k]
        spread = jnp.transpose(jnp.broadcast_to(total[0:1, :], (toks, toks)))
        scale[...] = lax.rsqrt(spread / D + 1e-05)

    state = {}

    def multiply(p):
        cols = slice(p * wide, (p + 1) * wide)
        for which, (load, weight) in enumerate(((gate_load, wgb), (up_load, wub))):
            load[p].wait()
            value = jnp.dot(xb[...], weight[:, cols], preferred_element_type=F32)
            for part in range(2):
                to = slice((2 * part + which) * sub, (2 * part + which + 1) * sub)
                at = slice(part * sub, (part + 1) * sub)
                keep[p, :, to] = value[0:half, at]
                send1[p, :, to] = value[half:toks, at].astype(BF)
        state["core", p] = push(send1.at[p], recv1.at[p], CORE)

    def fold_core(p):
        state["core", p].wait_recv()
        a, b = slice(0, wide), slice(wide, 2 * wide)
        two = 2 * blk

        def total(rows, cols):
            return keep[p, rows, cols] + recv1[p, rows, cols].astype(F32)

        send2[p, :, a] = total(slice(two, 2 * two), a).astype(BF)
        state["a2", p] = push(send2.at[p, :, a], recv2.at[p, :, a], XNBR)
        send2[p, 0:blk, b] = total(slice(blk, two), b).astype(BF)
        send2[p, blk:two, b] = total(slice(3 * blk, 4 * blk), b).astype(BF)
        state["b2", p] = push(send2.at[p, :, b], recv2.at[p, :, b], ZNBR)
        keep[p, 0:two, a] = total(slice(0, two), a)
        keep[p, 0:blk, b] = total(slice(0, blk), b)
        keep[p, two : 3 * blk, b] = total(slice(two, 3 * blk), b)

    def fold_second(p):
        a, b = slice(0, wide), slice(wide, 2 * wide)
        two = 2 * blk
        state["a2", p].wait_recv()
        send3[p, :, a] = (keep[p, blk:two, a] + recv2[p, blk:two, a].astype(F32)).astype(BF)
        state["a3", p] = push(send3.at[p, :, a], recv3.at[p, :, a], ZNBR)
        keep[p, 0:blk, a] += recv2[p, 0:blk, a].astype(F32)
        state["b2", p].wait_recv()
        send3[p, :, b] = (
            keep[p, two : 3 * blk, b] + recv2[p, blk:two, b].astype(F32)
        ).astype(BF)
        state["b3", p] = push(send3.at[p, :, b], recv3.at[p, :, b], XNBR)
        keep[p, 0:blk, b] += recv2[p, 0:blk, b].astype(F32)

    def activate(p):
        if p == 0:
            make_scale()
        factor = scale[pl.ds(token_block(0), blk), 0:1]
        for part, name in enumerate(("a3", "b3")):
            state[name, p].wait_recv()
            gates = slice(2 * part * sub, (2 * part + 1) * sub)
            ups = slice((2 * part + 1) * sub, (2 * part + 2) * sub)
            gate = (keep[p, 0:blk, gates] + recv3[p, :, gates].astype(F32)) * factor
            up = (keep[p, 0:blk, ups] + recv3[p, :, ups].astype(F32)) * factor
            hidden = gate / (1.0 + jnp.exp(-gate)) * up
            hb[p, 0:blk, part * sub : (part + 1) * sub] = hidden.astype(BF)
        state["hz", p] = push(hb.at[p, 0:blk], hb.at[p, blk : 2 * blk], ZNBR)
        state["hx", p] = push(hb.at[p, 0:blk], hb.at[p, 2 * blk : 3 * blk], XNBR)

    def relay(p):
        first, last = slice(0, sub), slice(sub, wide)
        far = slice(3 * blk, 4 * blk)
        state["hz", p].wait_recv()
        state["fx", p] = push(hb.at[p, blk : 2 * blk, first], hb.at[p, far, first], XNBR)
        state["hx", p].wait_recv()
        state["fz", p] = push(hb.at[p, 2 * blk : 3 * blk, last], hb.at[p, far, last], ZNBR)

    def share_core(p):
        state["fx", p].wait_recv()
        state["fz", p].wait_recv()
        state["hc", p] = push(hb.at[p, 0:half], hb.at[p, half:toks], CORE)

    def down(p):
        state["hc", p].wait_recv()
        rows = slice(p * wide, (p + 1) * wide)
        for side in (1, 0):
            cols = slice(side * out_w, (side + 1) * out_w)
            down_load[p][side].wait()
            value = jnp.dot(hb[p], wdb[rows, cols], preferred_element_type=F32)
            if p > 0:
                value = acc[:, cols] + value
            if p == PAIRS - 1 and side == 1:
                dsend[...] = value.astype(BF)
                state["down"] = push(dsend, drecv, OTHER)
            else:
                acc[:, cols] = value

    steps = (multiply, fold_core, fold_second, activate, relay, share_core, down)
    lag = (0, 1, 3, 4, 5, 6, 7)
    for tick in range(PAIRS + lag[-1]):
        for step, behind in zip(steps, lag):
            p = tick - behind
            if 0 <= p < PAIRS:
                step(p)
        if tick == 0:
            send_squares()

    state["down"].wait_recv()
    own_cols = pl.ds(pl.multiple_of(gr * out_w, out_w), out_w)
    for k in range(8):
        rows = slice(k * blk, (k + 1) * blk)
        value = stream[rows, own_cols] + acc[rows, 0:out_w] + drecv[rows, :].astype(F32)
        out[pl.ds(token_block(k), blk), :] = value.astype(BF)
    for copy in sent:
        copy.wait_send()


def fused(attn_out, residual_in, out_weight, norm_gain, gate_weight, up_weight, down_weight):
    toks, feat = attn_out.shape
    width = out_weight.shape[2]
    ff = gate_weight.shape[2]
    wide = ff // PAIRS
    half, blk = toks // 2, toks // 8
    vm = pltpu.VMEM
    scratch = [
        vm((width, ff), BF), vm((width, ff), BF), vm((ff, width), BF),
        vm((8, toks, feat), BF), vm((half, width), BF), vm((8, 128), F32),
        vm((toks, width), F32), vm((toks, width), BF), vm((toks, width), BF),
        vm((toks, width), F32), vm((toks, width), BF), vm((toks, width), F32),
        vm((8, toks), F32), vm((7, 8, toks), F32), vm((toks, toks), F32),
        vm((PAIRS, half, 2 * wide), F32),
        vm((PAIRS, half, 2 * wide), BF), vm((PAIRS, half, 2 * wide), BF),
        vm((PAIRS, 2 * blk, 2 * wide), BF), vm((PAIRS, 2 * blk, 2 * wide), BF),
        vm((PAIRS, blk, 2 * wide), BF), vm((PAIRS, blk, 2 * wide), BF),
        vm((PAIRS, toks, wide), BF),
        vm((toks, width // 2), BF), vm((toks, width // 2), BF),
        pltpu.SemaphoreType.DMA((40,)),
        pltpu.SemaphoreType.DMA((80,)), pltpu.SemaphoreType.DMA((80,)),
    ]
    flops = 2 * toks * width * (8 * feat + 3 * ff)
    traffic = 2 * width * (8 * feat + 3 * ff)
    result = pl.pallas_call(
        grid_kernel,
        out_shape=jax.ShapeDtypeStruct((toks, width // 2), BF),
        in_specs=[pl.BlockSpec(memory_space=pl.ANY)] * 7,
        out_specs=pl.BlockSpec(memory_space=pltpu.VMEM),
        scratch_shapes=scratch,
        compiler_params=pltpu.CompilerParams(
            collective_id=0, has_side_effects=True, vmem_limit_bytes=62 * 2**20
        ),
        cost_estimate=pl.CostEstimate(flops=flops, bytes_accessed=traffic, transcendentals=0),
    )(
        attn_out, residual_in, out_weight, norm_gain.reshape(-1, 128),
        gate_weight, up_weight, down_weight,
    )
    return result[:, None, :]


def solution(mesh):
    in_specs = (
        P("groups", "row"),
        P("row", "groups", None),
        P("row", None, None),
        P(),
        P("row", None, None),
        P("row", None, None),
        P("row", None, None),
    )
    out_specs = P("groups", "row", None)
    body = fused if mesh.shape["row"] == 2 * COLG else local
    return jax.shard_map(body, mesh=mesh, in_specs=in_specs, out_specs=out_specs, check_vma=False)
```

```python
import jax
import jax.numpy as jnp
from jax import lax
from jax.experimental import pallas as pl
from jax.experimental.pallas import tpu as pltpu
from jax.sharding import PartitionSpec as P

D = 8192
COLG = 8


def from_partner(value, axis, stride):
    mask = 2**stride
    pairs = [(source, source ^ mask) for source in range(lax.axis_size(axis))]
    return lax.ppermute(value, axis, pairs)


def gather_bits(value, dim, bit_list, device_pos, sender):
    for bit_pos in bit_list:
        incoming = sender(value, bit_pos)
        on_low = device_pos >> bit_pos & 1 == 0
        value = jnp.where(
            on_low, jnp.concatenate([value, incoming], dim), jnp.concatenate([incoming, value], dim)
        )
    return value


def reduce_bits(value, dim, bit_list, device_pos, sender):
    for bit_pos in reversed(bit_list):
        middle = value.shape[dim] // 2
        bottom = lax.slice_in_dim(value, 0, middle, axis=dim)
        top_part = lax.slice_in_dim(value, middle, 2 * middle, axis=dim)
        on_low = device_pos >> bit_pos & 1 == 0
        kept = jnp.where(on_low, bottom, top_part)
        outgoing = jnp.where(on_low, top_part, bottom)
        value = kept + sender(outgoing, bit_pos)
    return value


def sum_bits(value, bit_list, sender):
    for bit_pos in bit_list:
        value = value + sender(value, bit_pos)
    return value


def local(attn_out, residual_in, out_weight, norm_gain, gate_weight, up_weight, down_weight):
    all_bits = lax.axis_size("row").bit_length() - 1
    col_count = COLG.bit_length() - 1
    col_bits = list(range(col_count))
    row_bits = list(range(col_count, all_bits))
    device_pos = lax.axis_index("row")
    col_index = device_pos % COLG
    row_index = device_pos // COLG
    panel_in = gather_bits(
        attn_out,
        1,
        col_bits,
        device_pos,
        lambda block_piece, bit_pos: from_partner(block_piece, "row", bit_pos),
    )
    partial_proj = jnp.dot(panel_in, out_weight[0], preferred_element_type=jnp.float32)
    projected = reduce_bits(
        partial_proj,
        0,
        row_bits,
        device_pos,
        lambda block_piece, bit_pos: from_partner(block_piece, "row", bit_pos),
    )
    stream = (residual_in[0].astype(jnp.float32) + projected).astype(jnp.bfloat16)
    widened = stream.astype(jnp.float32)
    feat_cols = widened.shape[1]
    squares = jnp.sum(widened * widened, axis=-1)
    squares = sum_bits(
        squares, col_bits, lambda block_piece, bit_pos: from_partner(block_piece, "row", bit_pos)
    )
    mean_square = (squares / D)[:, None]
    gain_part = lax.dynamic_slice_in_dim(norm_gain, col_index * feat_cols, feat_cols)
    normed = (widened * lax.rsqrt(mean_square + 1e-05) * gain_part).astype(jnp.bfloat16)
    token_rows = gather_bits(
        normed,
        0,
        row_bits,
        device_pos,
        lambda block_piece, bit_pos: from_partner(block_piece, "row", bit_pos),
    )
    gate_vals = jnp.dot(token_rows, gate_weight[0], preferred_element_type=jnp.float32)
    up_vals = jnp.dot(token_rows, up_weight[0], preferred_element_type=jnp.float32)
    stacked = jnp.stack([gate_vals, up_vals])
    summed = reduce_bits(
        stacked,
        1,
        col_bits,
        device_pos,
        lambda block_piece, bit_pos: from_partner(block_piece, "row", bit_pos),
    )
    hidden = (jax.nn.silu(summed[0]) * summed[1]).astype(jnp.bfloat16)
    hidden_rows = gather_bits(
        hidden,
        0,
        col_bits,
        device_pos,
        lambda block_piece, bit_pos: from_partner(block_piece, "row", bit_pos),
    )
    partial_down = jnp.dot(hidden_rows, down_weight[0], preferred_element_type=jnp.float32)
    piece_width = feat_cols // 2 ** len(row_bits)
    stream_rows = gather_bits(
        stream,
        0,
        row_bits,
        device_pos,
        lambda block_piece, bit_pos: from_partner(block_piece, "row", bit_pos),
    )
    stream_piece = lax.dynamic_slice_in_dim(stream_rows, row_index * piece_width, piece_width, 1)
    down_piece = reduce_bits(
        partial_down,
        1,
        row_bits,
        device_pos,
        lambda block_piece, bit_pos: from_partner(block_piece, "row", bit_pos),
    )
    result = (stream_piece.astype(jnp.float32) + down_piece).astype(jnp.bfloat16)
    return result[:, None, :]


BF = jnp.bfloat16
F32 = jnp.float32
CORE, XNBR, ZNBR, OTHER = 1, 2, 4, 8
BATCHES = 2
SHARES = (3, 4, 4, 3)
CHUNKS = len(SHARES)


def chunks_of(units):
    one = units // sum(SHARES)
    starts = [one * sum(SHARES[:p]) for p in range(CHUNKS)]
    return [(start, one * share) for start, share in zip(starts, SHARES)]


def grid_kernel(
    attn, resid, wo, gain, wg, wu, wd, out,
    wgb, wub, wdb, panel, resb, gainb, pbuf, psend, precv, stream, xb, xs, acc,
    sq_out, sq_in, scale, keep, send1, recv1, send2, recv2, send3, recv3, hb,
    dsend, drecv, lsem, ssem, rsem,
):
    idx = lax.axis_index("row")
    core, xpos, zpos, gr = idx % 2, idx // 2 % 2, idx // 4 % 2, idx // 8
    bits = (core, xpos, zpos, gr)
    toks, width = pbuf.shape
    half = toks // BATCHES
    blk = half // 4
    two = 2 * blk
    feat = panel.shape[2]
    units = wgb.shape[2]
    out_w = width // 2
    chunks = chunks_of(units)
    slots = keep.shape[0]

    def peer(mask):
        moved = idx
        for pos, bit in enumerate(bits):
            if mask >> pos & 1:
                moved = moved + (1 - 2 * bit) * 2**pos
        return moved

    to_x, to_z = peer(XNBR) - idx, peer(ZNBR) - idx
    first_peer = idx + to_x + core * (to_z - to_x)
    second_peer = idx + to_z + core * (to_x - to_z)

    own_block = xpos * 2 + zpos
    flip_x, flip_z = 2 * (1 - 2 * xpos), 1 - 2 * zpos
    block_at = (
        own_block,
        own_block + flip_z + core * (flip_x - flip_z),
        own_block + flip_x + core * (flip_z - flip_x),
        own_block + flip_x + flip_z,
    )
    sibling_order = (0, 2, 1, 3)

    def token_rows(t, k):
        return pl.ds(pl.multiple_of(t * half + block_at[k] * blk, blk), blk)

    count = [0]
    sent = []
    local_count = [0]

    def push_to(src, dst, device):
        n = count[0]
        count[0] += 1
        copy = pltpu.make_async_remote_copy(
            src_ref=src, dst_ref=dst, send_sem=ssem.at[n], recv_sem=rsem.at[n],
            device_id={"row": device}, device_id_type=pl.DeviceIdType.MESH,
        )
        copy.start()
        sent.append(copy)
        return copy

    def push(src, dst, mask):
        return push_to(src, dst, peer(mask))

    def fetch(src, dst):
        n = local_count[0]
        local_count[0] += 1
        copy = pltpu.make_async_copy(src, dst, lsem.at[n])
        copy.start()
        return copy

    own_load = fetch(attn, panel.at[0])
    wo_load = {}
    for d in (0, 2, 4, 1, 6, 3, 5, 7):
        first = pl.multiple_of((peer(d) - gr * 8) * feat, feat)
        wo_load[d] = fetch(wo.at[0, pl.ds(first, feat), :], wdb.at[d * feat : (d + 1) * feat])
    res_load = fetch(resid.at[0], resb)
    gain_load = fetch(gain.at[pl.ds(pl.multiple_of(idx % 8 * 8, 8), 8), :], gainb)

    barrier = pltpu.get_barrier_semaphore()
    for mask in (1, 2, 3, 4, 5, 6, 7, 8):
        pl.semaphore_signal(
            barrier, inc=1, device_id={"row": peer(mask)}, device_id_type=pl.DeviceIdType.MESH
        )
    pl.semaphore_wait(barrier, 8)

    from_x = push(attn, panel.at[XNBR], XNBR)
    from_z = push(attn, panel.at[ZNBR], ZNBR)
    from_core = push(attn, panel.at[CORE], CORE)

    def project(d):
        return jnp.dot(
            panel[d], wdb[d * feat : (d + 1) * feat, :], preferred_element_type=F32
        )

    own_load.wait()
    wo_load[0].wait()
    pbuf[...] = project(0)
    from_x.wait_recv()
    mid = toks // 2
    diag_z = push(panel.at[2, 0:mid], panel.at[6, 0:mid], ZNBR)
    core_x = push(panel.at[2], panel.at[3], CORE)
    from_z.wait_recv()
    diag_x = push(panel.at[4, mid:toks], panel.at[6, mid:toks], XNBR)
    core_z = push(panel.at[4], panel.at[5], CORE)
    for d in (1, 2, 4, 3, 5, 6, 7):
        wo_load[d].wait()
    gate_load, up_load = [], []
    for start, sub in chunks:
        cols = slice(start, start + sub)
        for loads, weight, buf in ((gate_load, wg, wgb), (up_load, wu, wub)):
            both = []
            for side, owner in ((0, core), (1, 1 - core)):
                first = pl.multiple_of(owner * units + start, 256)
                both.append(fetch(weight.at[0, :, pl.ds(first, sub)], buf.at[side, :, cols]))
            loads.append(both)
    pbuf[...] += project(2)
    pbuf[...] += project(4)
    from_core.wait_recv()
    pbuf[...] += project(1)
    core_x.wait_recv()
    pbuf[...] += project(3)
    diag_z.wait_recv()
    diag_x.wait_recv()
    core_d = push(panel.at[6], panel.at[7], CORE)
    core_z.wait_recv()
    pbuf[...] += project(5)
    pbuf[...] += project(6)
    core_d.wait_recv()
    pbuf[...] += project(7)

    res_load.wait()
    mine = pl.ds(pl.multiple_of(gr * mid, mid), mid)
    pbuf[mine, :] += resb[...].astype(F32)
    from_other = []
    for t in range(BATCHES):
        rows = slice(t * half, (t + 1) * half)
        psend[rows, :] = pbuf[rows, :].astype(BF)
        from_other.append(push(psend.at[rows], precv.at[rows], OTHER))
    down_load = []
    for start, sub in chunks:
        both = []
        for side, owner in ((0, core), (1, 1 - core)):
            first = pl.multiple_of(owner * units + start, 256)
            to = 2 * start + side * sub
            for part, holder in ((0, gr), (1, 1 - gr)):
                cols = pl.ds(pl.multiple_of(holder * out_w, out_w), out_w)
                both.append(
                    fetch(
                        wd.at[0, pl.ds(first, sub), cols],
                        wdb.at[to : to + sub, part * out_w : (part + 1) * out_w],
                    )
                )
        down_load.append(both)
    gain_load.wait()
    gain_row = jnp.concatenate([gainb[j : j + 1, :] for j in range(8)], axis=1)

    sq_copies = {}

    def receive(t):
        rows = slice(t * half, (t + 1) * half)
        from_other[t].wait_recv()
        pbuf[rows, :] += precv[rows, :].astype(F32)
        for k in range(4):
            value = pbuf[token_rows(t, k), :]
            stream[t * half + k * blk : t * half + (k + 1) * blk, :] = value
            normed = (value * gain_row).astype(BF)
            j = sibling_order[k]
            xb[t * half + k * blk : t * half + (k + 1) * blk, :] = normed
            xs[t * half + j * blk : t * half + (j + 1) * blk, :] = normed

    def send_squares(t):
        total = pbuf[t * half : (t + 1) * half, :]
        total = jnp.sum(total * total, axis=1, keepdims=True)
        total = jnp.broadcast_to(total, (half, toks))
        sq_out[t] = jnp.transpose(jnp.concatenate([total] * BATCHES, axis=0))[0:8, :]
        sq_copies[t] = [
            push(sq_out.at[t], sq_in.at[t, mask - 1], mask) for mask in range(1, 8)
        ]

    def make_scale(t):
        total = sq_out[t]
        for copy in sq_copies[t]:
            copy.wait_recv()
        for k in range(7):
            total = total + sq_in[t, k]
        spread = jnp.transpose(jnp.broadcast_to(total[0:1, :], (toks, toks)))
        scale[t * half : (t + 1) * half, :] = lax.rsqrt(spread[0:half, :] / D + 1e-05)

    state = {}

    def multiply(i):
        t, p = divmod(i, CHUNKS)
        start, sub = chunks[p]
        if p == 0:
            receive(t)
        rows = slice(t * half, (t + 1) * half)
        cols = slice(start, start + sub)
        for side in (1, 0):
            for which, (load, weight) in enumerate(((gate_load, wgb), (up_load, wub))):
                if t == 0:
                    load[p][side].wait()
                source = xs if side else xb
                value = jnp.dot(
                    source[rows, :], weight[side, :, cols], preferred_element_type=F32
                )
                to = slice(which * sub, (which + 1) * sub)
                if side:
                    send1[i, :, to] = value.astype(BF)
                else:
                    keep[i % slots, :, to] = value
            if side:
                both = slice(0, 2 * sub)
                state["core", i] = push(send1.at[i, :, both], recv1.at[i, :, both], CORE)
        if p == 0:
            send_squares(t)

    def fold_core(i):
        both = slice(0, 2 * chunks[i % CHUNKS][1])
        state["core", i].wait_recv()
        s = i % slots
        send2[i, :, both] = (
            keep[s, two : 2 * two, both] + recv1[i, two : 2 * two, both].astype(F32)
        ).astype(BF)
        state["second", i] = push_to(send2.at[i, :, both], recv2.at[i, :, both], first_peer)
        keep[s, 0:two, both] += recv1[i, 0:two, both].astype(F32)

    def fold_second(i):
        both = slice(0, 2 * chunks[i % CHUNKS][1])
        state["second", i].wait_recv()
        s = i % slots
        send3[i, :, both] = (
            keep[s, blk:two, both] + recv2[i, blk:two, both].astype(F32)
        ).astype(BF)
        state["third", i] = push_to(send3.at[i, :, both], recv3.at[i, :, both], second_peer)
        keep[s, 0:blk, both] += recv2[i, 0:blk, both].astype(F32)

    def share_block(i, k):
        cols = slice(0, chunks[i % CHUNKS][1])
        sub = chunks[i % CHUNKS][1]
        j = sibling_order[k]
        state["hc", i, k] = push(
            hb.at[i, k * blk : (k + 1) * blk, cols],
            hb.at[i, j * blk : (j + 1) * blk, sub : 2 * sub],
            CORE,
        )

    def activate(i):
        t, p = divmod(i, CHUNKS)
        sub = chunks[p][1]
        if p == 0:
            make_scale(t)
        s = i % slots
        state["third", i].wait_recv()
        factor = scale[token_rows(t, 0), 0:1]
        gate = (keep[s, 0:blk, 0:sub] + recv3[i, :, 0:sub].astype(F32)) * factor
        up = (keep[s, 0:blk, sub : 2 * sub] + recv3[i, :, sub : 2 * sub].astype(F32)) * factor
        hb[i, 0:blk, 0:sub] = (gate / (1.0 + jnp.exp(-gate)) * up).astype(BF)
        own = hb.at[i, 0:blk, 0:sub]
        state["h1", i] = push_to(own, hb.at[i, blk:two, 0:sub], second_peer)
        state["h2", i] = push_to(own, hb.at[i, two : 3 * blk, 0:sub], first_peer)
        share_block(i, 0)

    def relay(i):
        sub = chunks[i % CHUNKS][1]
        state["h1", i].wait_recv()
        state["h3", i] = push_to(
            hb.at[i, blk:two, 0:sub], hb.at[i, 3 * blk : 4 * blk, 0:sub], first_peer
        )
        share_block(i, 1)
        state["h2", i].wait_recv()
        share_block(i, 2)

    def share_last(i):
        state["h3", i].wait_recv()
        share_block(i, 3)

    def down(i):
        t, p = divmod(i, CHUNKS)
        start, sub = chunks[p]
        for k in range(4):
            state["hc", i, k].wait_recv()
        if t == 0:
            for load in down_load[p]:
                load.wait()
        rows = slice(2 * start, 2 * start + 2 * sub)
        batch = slice(t * half, (t + 1) * half)
        for part in (1, 0):
            cols = slice(part * out_w, (part + 1) * out_w)
            value = jnp.dot(
                hb[i, :, 0 : 2 * sub], wdb[rows, cols], preferred_element_type=F32
            )
            if p > 0:
                value = acc[batch, cols] + value
            if p == CHUNKS - 1 and part == 1:
                dsend[batch, :] = value.astype(BF)
                state["down", t] = push(dsend.at[batch], drecv.at[batch], OTHER)
            else:
                acc[batch, cols] = value

    steps = (multiply, fold_core, fold_second, activate, relay, share_last, down)
    items = BATCHES * CHUNKS
    for tick in range(items + len(steps) - 1):
        for behind, step in enumerate(steps):
            if 0 <= tick - behind < items:
                step(tick - behind)

    own_cols = pl.ds(pl.multiple_of(gr * out_w, out_w), out_w)
    for t in range(BATCHES):
        state["down", t].wait_recv()
        for k in range(4):
            rows = slice(t * half + k * blk, t * half + (k + 1) * blk)
            value = stream[rows, own_cols] + acc[rows, 0:out_w] + drecv[rows, :].astype(F32)
            out[token_rows(t, k), :] = value.astype(BF)
    for copy in sent:
        copy.wait_send()


def fused(attn_out, residual_in, out_weight, norm_gain, gate_weight, up_weight, down_weight):
    toks, feat = attn_out.shape
    width = out_weight.shape[2]
    ff = gate_weight.shape[2]
    half = toks // BATCHES
    blk = half // 4
    items = BATCHES * CHUNKS
    most = 2 * max(sub for start, sub in chunks_of(ff // 2))
    vm = pltpu.VMEM
    scratch = [
        vm((2, width, ff // 2), BF), vm((2, width, ff // 2), BF), vm((ff, width), BF),
        vm((8, toks, feat), BF), vm((toks // 2, width), BF), vm((8, 128), F32),
        vm((toks, width), F32), vm((toks, width), BF), vm((toks, width), BF),
        vm((toks, width), F32), vm((toks, width), BF), vm((toks, width), BF),
        vm((toks, width), F32),
        vm((BATCHES, 8, toks), F32), vm((BATCHES, 7, 8, toks), F32), vm((toks, toks), F32),
        vm((4, half, most), F32),
        vm((items, half, most), BF), vm((items, half, most), BF),
        vm((items, 2 * blk, most), BF), vm((items, 2 * blk, most), BF),
        vm((items, blk, most), BF), vm((items, blk, most), BF),
        vm((items, half, most), BF),
        vm((toks, width // 2), BF), vm((toks, width // 2), BF),
        pltpu.SemaphoreType.DMA((64,)),
        pltpu.SemaphoreType.DMA((128,)), pltpu.SemaphoreType.DMA((128,)),
    ]
    flops = 2 * toks * width * (8 * feat + 3 * ff)
    traffic = 2 * width * (8 * feat + 3 * ff)
    result = pl.pallas_call(
        grid_kernel,
        out_shape=jax.ShapeDtypeStruct((toks, width // 2), BF),
        in_specs=[pl.BlockSpec(memory_space=pl.ANY)] * 7,
        out_specs=pl.BlockSpec(memory_space=pltpu.VMEM),
        scratch_shapes=scratch,
        compiler_params=pltpu.CompilerParams(
            collective_id=0, has_side_effects=True, vmem_limit_bytes=62 * 2**20
        ),
        cost_estimate=pl.CostEstimate(flops=flops, bytes_accessed=traffic, transcendentals=0),
    )(
        attn_out, residual_in, out_weight, norm_gain.reshape(-1, 128),
        gate_weight, up_weight, down_weight,
    )
    return result[:, None, :]


def solution(mesh):
    in_specs = (
        P("groups", "row"),
        P("row", "groups", None),
        P("row", None, None),
        P(),
        P("row", None, None),
        P("row", None, None),
        P("row", None, None),
    )
    out_specs = P("groups", "row", None)
    body = fused if mesh.shape["row"] == 2 * COLG else local
    return jax.shard_map(body, mesh=mesh, in_specs=in_specs, out_specs=out_specs, check_vma=False)
```

```python
import jax
import jax.numpy as jnp
from jax import lax
from jax.experimental import pallas as pl
from jax.experimental.pallas import tpu as pltpu
from jax.sharding import PartitionSpec as P

D = 8192
COLG = 8


def from_partner(value, axis, stride):
    mask = 2**stride
    pairs = [(source, source ^ mask) for source in range(lax.axis_size(axis))]
    return lax.ppermute(value, axis, pairs)


def gather_bits(value, dim, bit_list, device_pos, sender):
    for bit_pos in bit_list:
        incoming = sender(value, bit_pos)
        on_low = device_pos >> bit_pos & 1 == 0
        value = jnp.where(
            on_low, jnp.concatenate([value, incoming], dim), jnp.concatenate([incoming, value], dim)
        )
    return value


def reduce_bits(value, dim, bit_list, device_pos, sender):
    for bit_pos in reversed(bit_list):
        middle = value.shape[dim] // 2
        bottom = lax.slice_in_dim(value, 0, middle, axis=dim)
        top_part = lax.slice_in_dim(value, middle, 2 * middle, axis=dim)
        on_low = device_pos >> bit_pos & 1 == 0
        kept = jnp.where(on_low, bottom, top_part)
        outgoing = jnp.where(on_low, top_part, bottom)
        value = kept + sender(outgoing, bit_pos)
    return value


def sum_bits(value, bit_list, sender):
    for bit_pos in bit_list:
        value = value + sender(value, bit_pos)
    return value


def local(attn_out, residual_in, out_weight, norm_gain, gate_weight, up_weight, down_weight):
    all_bits = lax.axis_size("row").bit_length() - 1
    col_count = COLG.bit_length() - 1
    col_bits = list(range(col_count))
    row_bits = list(range(col_count, all_bits))
    device_pos = lax.axis_index("row")
    col_index = device_pos % COLG
    row_index = device_pos // COLG
    panel_in = gather_bits(
        attn_out,
        1,
        col_bits,
        device_pos,
        lambda block_piece, bit_pos: from_partner(block_piece, "row", bit_pos),
    )
    partial_proj = jnp.dot(panel_in, out_weight[0], preferred_element_type=jnp.float32)
    projected = reduce_bits(
        partial_proj,
        0,
        row_bits,
        device_pos,
        lambda block_piece, bit_pos: from_partner(block_piece, "row", bit_pos),
    )
    stream = (residual_in[0].astype(jnp.float32) + projected).astype(jnp.bfloat16)
    widened = stream.astype(jnp.float32)
    feat_cols = widened.shape[1]
    squares = jnp.sum(widened * widened, axis=-1)
    squares = sum_bits(
        squares, col_bits, lambda block_piece, bit_pos: from_partner(block_piece, "row", bit_pos)
    )
    mean_square = (squares / D)[:, None]
    gain_part = lax.dynamic_slice_in_dim(norm_gain, col_index * feat_cols, feat_cols)
    normed = (widened * lax.rsqrt(mean_square + 1e-05) * gain_part).astype(jnp.bfloat16)
    token_rows = gather_bits(
        normed,
        0,
        row_bits,
        device_pos,
        lambda block_piece, bit_pos: from_partner(block_piece, "row", bit_pos),
    )
    gate_vals = jnp.dot(token_rows, gate_weight[0], preferred_element_type=jnp.float32)
    up_vals = jnp.dot(token_rows, up_weight[0], preferred_element_type=jnp.float32)
    stacked = jnp.stack([gate_vals, up_vals])
    summed = reduce_bits(
        stacked,
        1,
        col_bits,
        device_pos,
        lambda block_piece, bit_pos: from_partner(block_piece, "row", bit_pos),
    )
    hidden = (jax.nn.silu(summed[0]) * summed[1]).astype(jnp.bfloat16)
    hidden_rows = gather_bits(
        hidden,
        0,
        col_bits,
        device_pos,
        lambda block_piece, bit_pos: from_partner(block_piece, "row", bit_pos),
    )
    partial_down = jnp.dot(hidden_rows, down_weight[0], preferred_element_type=jnp.float32)
    piece_width = feat_cols // 2 ** len(row_bits)
    stream_rows = gather_bits(
        stream,
        0,
        row_bits,
        device_pos,
        lambda block_piece, bit_pos: from_partner(block_piece, "row", bit_pos),
    )
    stream_piece = lax.dynamic_slice_in_dim(stream_rows, row_index * piece_width, piece_width, 1)
    down_piece = reduce_bits(
        partial_down,
        1,
        row_bits,
        device_pos,
        lambda block_piece, bit_pos: from_partner(block_piece, "row", bit_pos),
    )
    result = (stream_piece.astype(jnp.float32) + down_piece).astype(jnp.bfloat16)
    return result[:, None, :]


BF = jnp.bfloat16
F32 = jnp.float32
CORE, XNBR, ZNBR, OTHER = 1, 2, 4, 8
PIECES = 4
SHARES = (4, 4, 4, 2)
CHUNKS = len(SHARES)


def chunks_of(units):
    one = units // sum(SHARES)
    starts = [one * sum(SHARES[:p]) for p in range(CHUNKS)]
    return [(start, one * share) for start, share in zip(starts, SHARES)]


def grid_kernel(
    attn, resid, wo, gain, wg, wu, wd, own_out, other_out,
    wgb, wub, wdb, panel, resb, gainb, pbuf, psend, precv, xb, xs, acc,
    sq_out, sq_in, scale, keep, give, send1, recv1, send2, recv2, send3, recv3, hb,
    dsend, lsem, ssem, rsem,
):
    idx = lax.axis_index("row")
    core, xpos, zpos, gr = idx % 2, idx // 2 % 2, idx // 4 % 2, idx // 8
    bits = (core, xpos, zpos, gr)
    toks, width = pbuf.shape
    blk = toks // 4
    two = 2 * blk
    feat = panel.shape[2]
    units = wgb.shape[2]
    out_w = width // 2
    chunks = chunks_of(units)
    piece = width // PIECES

    def peer(mask):
        moved = idx
        for pos, bit in enumerate(bits):
            if mask >> pos & 1:
                moved = moved + (1 - 2 * bit) * 2**pos
        return moved

    to_x, to_z = peer(XNBR) - idx, peer(ZNBR) - idx
    first_peer = idx + to_x + core * (to_z - to_x)
    second_peer = idx + to_z + core * (to_x - to_z)

    own_block = xpos * 2 + zpos
    flip_x, flip_z = 2 * (1 - 2 * xpos), 1 - 2 * zpos
    block_at = (
        own_block,
        own_block + flip_z + core * (flip_x - flip_z),
        own_block + flip_x + core * (flip_z - flip_x),
        own_block + flip_x + flip_z,
    )
    sibling_order = (0, 2, 1, 3)

    def token_rows(k):
        return pl.ds(pl.multiple_of(block_at[k] * blk, blk), blk)

    def feats(q):
        return slice(q * piece, (q + 1) * piece)

    count = [0]
    sent = []
    local_count = [0]

    def push_to(src, dst, device):
        n = count[0]
        count[0] += 1
        copy = pltpu.make_async_remote_copy(
            src_ref=src, dst_ref=dst, send_sem=ssem.at[n], recv_sem=rsem.at[n],
            device_id={"row": device}, device_id_type=pl.DeviceIdType.MESH,
        )
        copy.start()
        sent.append(copy)
        return copy

    def push(src, dst, mask):
        return push_to(src, dst, peer(mask))

    def fetch(src, dst):
        n = local_count[0]
        local_count[0] += 1
        copy = pltpu.make_async_copy(src, dst, lsem.at[n])
        copy.start()
        return copy

    own_load = fetch(attn, panel.at[0])
    wo_load = {}
    for d in (0, 2, 4, 1, 6, 3, 5, 7):
        first = pl.multiple_of((peer(d) - gr * 8) * feat, feat)
        wo_load[d] = fetch(wo.at[0, pl.ds(first, feat), :], wdb.at[d * feat : (d + 1) * feat])
    res_load = fetch(resid.at[0], resb)
    gain_load = fetch(gain.at[pl.ds(pl.multiple_of(idx % 8 * 8, 8), 8), :], gainb)

    barrier = pltpu.get_barrier_semaphore()
    for mask in (1, 2, 3, 4, 5, 6, 7, 8):
        pl.semaphore_signal(
            barrier, inc=1, device_id={"row": peer(mask)}, device_id_type=pl.DeviceIdType.MESH
        )
    pl.semaphore_wait(barrier, 8)

    gate_up_load = {}

    def load_gate_up(q):
        for which, (weight, buf) in enumerate(((wg, wgb), (wu, wub))):
            for side, owner in ((0, core), (1, 1 - core)):
                cols = pl.ds(pl.multiple_of(owner * units, units), units)
                gate_up_load[q, which, side] = fetch(
                    weight.at[0, feats(q), cols], buf.at[side, feats(q), :]
                )

    from_x = push(attn, panel.at[XNBR], XNBR)
    from_z = push(attn, panel.at[ZNBR], ZNBR)
    from_core = push(attn, panel.at[CORE], CORE)

    def project(d):
        return jnp.dot(
            panel[d], wdb[d * feat : (d + 1) * feat, :], preferred_element_type=F32
        )

    load_gate_up(0)
    own_load.wait()
    wo_load[0].wait()
    pbuf[...] = project(0)
    from_x.wait_recv()
    mid = toks // 2
    diag_z = push(panel.at[2, 0:mid], panel.at[6, 0:mid], ZNBR)
    core_x = push(panel.at[2], panel.at[3], CORE)
    from_z.wait_recv()
    diag_x = push(panel.at[4, mid:toks], panel.at[6, mid:toks], XNBR)
    core_z = push(panel.at[4], panel.at[5], CORE)
    for d in (1, 2, 4, 3, 5, 6, 7):
        wo_load[d].wait()
    for q in range(1, PIECES):
        load_gate_up(q)
    pbuf[...] += project(2)
    pbuf[...] += project(4)
    from_core.wait_recv()
    pbuf[...] += project(1)
    core_x.wait_recv()
    pbuf[...] += project(3)
    diag_z.wait_recv()
    diag_x.wait_recv()
    core_d = push(panel.at[6], panel.at[7], CORE)
    core_z.wait_recv()
    pbuf[...] += project(5)
    pbuf[...] += project(6)
    core_d.wait_recv()

    res_load.wait()
    mine = pl.ds(pl.multiple_of(gr * mid, mid), mid)
    pbuf[mine, :] += resb[...].astype(F32)
    from_other = []
    for q in range(PIECES):
        value = pbuf[:, feats(q)] + jnp.dot(
            panel[7], wdb[7 * feat : 8 * feat, feats(q)], preferred_element_type=F32
        )
        pbuf[:, feats(q)] = value
        psend[:, feats(q)] = value.astype(BF)
        from_other.append(push(psend.at[:, feats(q)], precv.at[:, feats(q)], OTHER))
    down_load = []
    for start, sub in chunks:
        both = []
        for side, owner in ((0, core), (1, 1 - core)):
            first = pl.multiple_of(owner * units + start, 256)
            to = 2 * start + side * sub
            for part, holder in ((0, gr), (1, 1 - gr)):
                cols = pl.ds(pl.multiple_of(holder * out_w, out_w), out_w)
                both.append(
                    fetch(
                        wd.at[0, pl.ds(first, sub), cols],
                        wdb.at[to : to + sub, part * out_w : (part + 1) * out_w],
                    )
                )
        down_load.append(both)
    gain_load.wait()
    gain_row = jnp.concatenate([gainb[j : j + 1, :] for j in range(8)], axis=1)

    sq_copies = []

    def receive(q):
        cols = feats(q)
        from_other[q].wait_recv()
        pbuf[:, cols] += precv[:, cols].astype(F32)
        for k in range(4):
            normed = (pbuf[token_rows(k), cols] * gain_row[:, cols]).astype(BF)
            j = sibling_order[k]
            xb[k * blk : (k + 1) * blk, cols] = normed
            xs[j * blk : (j + 1) * blk, cols] = normed

    def send_squares():
        total = pbuf[...]
        total = jnp.sum(total * total, axis=1, keepdims=True)
        sq_out[...] = jnp.transpose(jnp.broadcast_to(total, (toks, toks)))[0:8, :]
        for mask in range(1, 8):
            sq_copies.append(push(sq_out, sq_in.at[mask - 1], mask))

    def make_scale():
        total = sq_out[...]
        for copy in sq_copies:
            copy.wait_recv()
        for k in range(7):
            total = total + sq_in[k]
        spread = jnp.transpose(jnp.broadcast_to(total[0:1, :], (toks, toks)))
        scale[...] = lax.rsqrt(spread / D + 1e-05)

    state = {}

    def columns(p):
        start, sub = chunks[p]
        return slice(2 * start, 2 * start + 2 * sub)

    def product(p, q, side, which):
        start, sub = chunks[p]
        source, weight = (xs if side else xb), (wub if which else wgb)
        return jnp.dot(
            source[:, feats(q)],
            weight[side, feats(q), start : start + sub],
            preferred_element_type=F32,
        )

    def add_piece(q):
        for p, (start, sub) in enumerate(chunks):
            for side, buf in ((1, give), (0, keep)):
                for which in range(2):
                    if p == 0:
                        gate_up_load[q, which, side].wait()
                    to = slice(2 * start + which * sub, 2 * start + (which + 1) * sub)
                    value = product(p, q, side, which)
                    buf[:, to] = value if q == 0 else buf[:, to] + value

    def multiply(p):
        start, sub = chunks[p]
        q = PIECES - 1
        for side in (1, 0):
            for which in range(2):
                if p == 0:
                    gate_up_load[q, which, side].wait()
                to = slice(2 * start + which * sub, 2 * start + (which + 1) * sub)
                value = product(p, q, side, which)
                if side:
                    send1[:, to] = (give[:, to] + value).astype(BF)
                else:
                    keep[:, to] += value
            if side:
                both = columns(p)
                state["core", p] = push(send1.at[:, both], recv1.at[:, both], CORE)

    def fold_core(p):
        both = columns(p)
        state["core", p].wait_recv()
        send2[:, both] = (
            keep[two : 2 * two, both] + recv1[two : 2 * two, both].astype(F32)
        ).astype(BF)
        state["second", p] = push_to(send2.at[:, both], recv2.at[:, both], first_peer)
        keep[0:two, both] += recv1[0:two, both].astype(F32)

    def fold_second(p):
        both = columns(p)
        state["second", p].wait_recv()
        send3[:, both] = (keep[blk:two, both] + recv2[blk:two, both].astype(F32)).astype(BF)
        state["third", p] = push_to(send3.at[:, both], recv3.at[:, both], second_peer)
        keep[0:blk, both] += recv2[0:blk, both].astype(F32)

    def own_units(p):
        start, sub = chunks[p]
        return slice(2 * start, 2 * start + sub)

    def sibling_units(p):
        start, sub = chunks[p]
        return slice(2 * start + sub, 2 * start + 2 * sub)

    def share_block(p, k):
        j = sibling_order[k]
        state["hc", p, k] = push(
            hb.at[k * blk : (k + 1) * blk, own_units(p)],
            hb.at[j * blk : (j + 1) * blk, sibling_units(p)],
            CORE,
        )

    def activate(p):
        if p == 0:
            make_scale()
        cols, ups = own_units(p), sibling_units(p)
        state["third", p].wait_recv()
        factor = scale[token_rows(0), 0:1]
        gate = (keep[0:blk, cols] + recv3[:, cols].astype(F32)) * factor
        up = (keep[0:blk, ups] + recv3[:, ups].astype(F32)) * factor
        hb[0:blk, cols] = (gate / (1.0 + jnp.exp(-gate)) * up).astype(BF)
        own = hb.at[0:blk, cols]
        state["h1", p] = push_to(own, hb.at[blk:two, cols], second_peer)
        state["h2", p] = push_to(own, hb.at[two : 3 * blk, cols], first_peer)
        share_block(p, 0)

    def relay(p):
        cols = own_units(p)
        state["h1", p].wait_recv()
        state["h3", p] = push_to(
            hb.at[blk:two, cols], hb.at[3 * blk : 4 * blk, cols], first_peer
        )
        share_block(p, 1)
        state["h2", p].wait_recv()
        share_block(p, 2)

    def share_last(p):
        state["h3", p].wait_recv()
        share_block(p, 3)

    def down(p):
        for k in range(4):
            state["hc", p, k].wait_recv()
        for load in down_load[p]:
            load.wait()
        for part in (1, 0):
            cols = slice(part * out_w, (part + 1) * out_w)
            value = jnp.dot(hb[:, columns(p)], wdb[columns(p), cols], preferred_element_type=F32)
            if p > 0:
                value = acc[:, cols] + value
            if p == CHUNKS - 1 and part == 1:
                dsend[...] = value.astype(BF)
                for k in range(4):
                    state["down", k] = push(
                        dsend.at[k * blk : (k + 1) * blk], other_out.at[token_rows(k)], OTHER
                    )
            else:
                acc[:, cols] = value

    for q in range(PIECES - 1):
        receive(q)
        add_piece(q)
    receive(PIECES - 1)
    steps = (multiply, fold_core, fold_second, activate, relay, share_last, down)
    lag = (0, 1, 4, 5, 6, 7, 8)
    for tick in range(CHUNKS + lag[-1]):
        for behind, step in zip(lag, steps):
            if 0 <= tick - behind < CHUNKS:
                step(tick - behind)
        if tick == 1:
            send_squares()

    own_cols = pl.ds(pl.multiple_of(gr * out_w, out_w), out_w)
    for k in range(4):
        rows = slice(k * blk, (k + 1) * blk)
        own_out[token_rows(k), :] = pbuf[token_rows(k), own_cols] + acc[rows, 0:out_w]
    for k in range(4):
        state["down", k].wait_recv()
    for copy in sent:
        copy.wait_send()


def fused(attn_out, residual_in, out_weight, norm_gain, gate_weight, up_weight, down_weight):
    toks, feat = attn_out.shape
    width = out_weight.shape[2]
    ff = gate_weight.shape[2]
    blk = toks // 4
    vm = pltpu.VMEM
    scratch = [
        vm((2, width, ff // 2), BF), vm((2, width, ff // 2), BF), vm((ff, width), BF),
        vm((8, toks, feat), BF), vm((toks // 2, width), BF), vm((8, 128), F32),
        vm((toks, width), F32), vm((toks, width), BF), vm((toks, width), BF),
        vm((toks, width), BF), vm((toks, width), BF), vm((toks, width), F32),
        vm((8, toks), F32), vm((7, 8, toks), F32), vm((toks, toks), F32),
        vm((toks, ff), F32), vm((toks, ff), F32), vm((toks, ff), BF), vm((toks, ff), BF),
        vm((2 * blk, ff), BF), vm((2 * blk, ff), BF),
        vm((blk, ff), BF), vm((blk, ff), BF),
        vm((toks, ff), BF), vm((toks, width // 2), BF),
        pltpu.SemaphoreType.DMA((64,)),
        pltpu.SemaphoreType.DMA((96,)), pltpu.SemaphoreType.DMA((96,)),
    ]
    flops = 2 * toks * width * (8 * feat + 3 * ff)
    traffic = 2 * width * (8 * feat + 3 * ff)
    own, other = pl.pallas_call(
        grid_kernel,
        out_shape=(
            jax.ShapeDtypeStruct((toks, width // 2), F32),
            jax.ShapeDtypeStruct((toks, width // 2), BF),
        ),
        in_specs=[pl.BlockSpec(memory_space=pl.ANY)] * 7,
        out_specs=(
            pl.BlockSpec(memory_space=pltpu.VMEM), pl.BlockSpec(memory_space=pl.ANY)
        ),
        scratch_shapes=scratch,
        compiler_params=pltpu.CompilerParams(
            collective_id=0, has_side_effects=True, vmem_limit_bytes=62 * 2**20
        ),
        cost_estimate=pl.CostEstimate(flops=flops, bytes_accessed=traffic, transcendentals=0),
    )(
        attn_out, residual_in, out_weight, norm_gain.reshape(-1, 128),
        gate_weight, up_weight, down_weight,
    )
    return (own + other.astype(F32)).astype(BF)[:, None, :]


def solution(mesh):
    in_specs = (
        P("groups", "row"),
        P("row", "groups", None),
        P("row", None, None),
        P(),
        P("row", None, None),
        P("row", None, None),
        P("row", None, None),
    )
    out_specs = P("groups", "row", None)
    body = fused if mesh.shape["row"] == 2 * COLG else local
    return jax.shard_map(body, mesh=mesh, in_specs=in_specs, out_specs=out_specs, check_vma=False)
```

```python
import jax
import jax.numpy as jnp
from jax import lax
from jax.experimental import pallas as pl
from jax.experimental.pallas import tpu as pltpu
from jax.sharding import PartitionSpec as P

D = 8192
COLG = 8


def from_partner(value, axis, stride):
    mask = 2**stride
    pairs = [(source, source ^ mask) for source in range(lax.axis_size(axis))]
    return lax.ppermute(value, axis, pairs)


def gather_bits(value, dim, bit_list, device_pos, sender):
    for bit_pos in bit_list:
        incoming = sender(value, bit_pos)
        on_low = device_pos >> bit_pos & 1 == 0
        value = jnp.where(
            on_low, jnp.concatenate([value, incoming], dim), jnp.concatenate([incoming, value], dim)
        )
    return value


def reduce_bits(value, dim, bit_list, device_pos, sender):
    for bit_pos in reversed(bit_list):
        middle = value.shape[dim] // 2
        bottom = lax.slice_in_dim(value, 0, middle, axis=dim)
        top_part = lax.slice_in_dim(value, middle, 2 * middle, axis=dim)
        on_low = device_pos >> bit_pos & 1 == 0
        kept = jnp.where(on_low, bottom, top_part)
        outgoing = jnp.where(on_low, top_part, bottom)
        value = kept + sender(outgoing, bit_pos)
    return value


def sum_bits(value, bit_list, sender):
    for bit_pos in bit_list:
        value = value + sender(value, bit_pos)
    return value


def local(attn_out, residual_in, out_weight, norm_gain, gate_weight, up_weight, down_weight):
    all_bits = lax.axis_size("row").bit_length() - 1
    col_count = COLG.bit_length() - 1
    col_bits = list(range(col_count))
    row_bits = list(range(col_count, all_bits))
    device_pos = lax.axis_index("row")
    col_index = device_pos % COLG
    row_index = device_pos // COLG
    panel_in = gather_bits(
        attn_out,
        1,
        col_bits,
        device_pos,
        lambda block_piece, bit_pos: from_partner(block_piece, "row", bit_pos),
    )
    partial_proj = jnp.dot(panel_in, out_weight[0], preferred_element_type=jnp.float32)
    projected = reduce_bits(
        partial_proj,
        0,
        row_bits,
        device_pos,
        lambda block_piece, bit_pos: from_partner(block_piece, "row", bit_pos),
    )
    stream = (residual_in[0].astype(jnp.float32) + projected).astype(jnp.bfloat16)
    widened = stream.astype(jnp.float32)
    feat_cols = widened.shape[1]
    squares = jnp.sum(widened * widened, axis=-1)
    squares = sum_bits(
        squares, col_bits, lambda block_piece, bit_pos: from_partner(block_piece, "row", bit_pos)
    )
    mean_square = (squares / D)[:, None]
    gain_part = lax.dynamic_slice_in_dim(norm_gain, col_index * feat_cols, feat_cols)
    normed = (widened * lax.rsqrt(mean_square + 1e-05) * gain_part).astype(jnp.bfloat16)
    token_rows = gather_bits(
        normed,
        0,
        row_bits,
        device_pos,
        lambda block_piece, bit_pos: from_partner(block_piece, "row", bit_pos),
    )
    gate_vals = jnp.dot(token_rows, gate_weight[0], preferred_element_type=jnp.float32)
    up_vals = jnp.dot(token_rows, up_weight[0], preferred_element_type=jnp.float32)
    stacked = jnp.stack([gate_vals, up_vals])
    summed = reduce_bits(
        stacked,
        1,
        col_bits,
        device_pos,
        lambda block_piece, bit_pos: from_partner(block_piece, "row", bit_pos),
    )
    hidden = (jax.nn.silu(summed[0]) * summed[1]).astype(jnp.bfloat16)
    hidden_rows = gather_bits(
        hidden,
        0,
        col_bits,
        device_pos,
        lambda block_piece, bit_pos: from_partner(block_piece, "row", bit_pos),
    )
    partial_down = jnp.dot(hidden_rows, down_weight[0], preferred_element_type=jnp.float32)
    piece_width = feat_cols // 2 ** len(row_bits)
    stream_rows = gather_bits(
        stream,
        0,
        row_bits,
        device_pos,
        lambda block_piece, bit_pos: from_partner(block_piece, "row", bit_pos),
    )
    stream_piece = lax.dynamic_slice_in_dim(stream_rows, row_index * piece_width, piece_width, 1)
    down_piece = reduce_bits(
        partial_down,
        1,
        row_bits,
        device_pos,
        lambda block_piece, bit_pos: from_partner(block_piece, "row", bit_pos),
    )
    result = (stream_piece.astype(jnp.float32) + down_piece).astype(jnp.bfloat16)
    return result[:, None, :]


BF = jnp.bfloat16
F32 = jnp.float32
CORE, XNBR, ZNBR, OTHER = 1, 2, 4, 8
BATCHES = 2
SHARES = (3, 4)
ITEMS = ((0, 0), (0, 1), (1, 1), (1, 0))


def chunks_of(units):
    one = units // sum(SHARES)
    return [(one * sum(SHARES[:p]), one * share) for p, share in enumerate(SHARES)]


def columns_of(units):
    spans, start = [], 0
    for t, p in ITEMS:
        wide = 2 * chunks_of(units)[p][1]
        spans.append(slice(start, start + wide))
        start += wide
    return spans


def grid_kernel(
    attn, resid, wo, gain, wg, wu, wd, own_out, other_out,
    wgb, wub, wdb, panel, resb, gainb, pbuf, psend, precv, xb, acc,
    sq_out, sq_in, scale, keep, send1, recv1, send2, recv2, send3, recv3, hb,
    dsend, lsem, ssem, rsem,
):
    idx = lax.axis_index("row")
    core, xpos, zpos, gr = idx % 2, idx // 2 % 2, idx // 4 % 2, idx // 8
    bits = (core, xpos, zpos, gr)
    toks, width = pbuf.shape
    half = toks // BATCHES
    blk = half // 4
    two = 2 * blk
    feat = panel.shape[2]
    units = wgb.shape[2]
    out_w = width // 2
    chunks = chunks_of(units)
    spans = columns_of(units)

    def peer(mask):
        moved = idx
        for pos, bit in enumerate(bits):
            if mask >> pos & 1:
                moved = moved + (1 - 2 * bit) * 2**pos
        return moved

    own_block = xpos * 2 + zpos
    flip_x, flip_z = 2 * (1 - 2 * xpos), 1 - 2 * zpos
    block_at = (
        own_block, own_block + flip_z, own_block + flip_x, own_block + flip_x + flip_z
    )

    def token_rows(t, k):
        return pl.ds(pl.multiple_of(t * half + block_at[k] * blk, blk), blk)

    def batch_rows(t):
        return slice(t * half, (t + 1) * half)

    count = [0]
    sent = []
    local_count = [0]

    def push(src, dst, mask):
        n = count[0]
        count[0] += 1
        copy = pltpu.make_async_remote_copy(
            src_ref=src, dst_ref=dst, send_sem=ssem.at[n], recv_sem=rsem.at[n],
            device_id={"row": peer(mask)}, device_id_type=pl.DeviceIdType.MESH,
        )
        copy.start()
        sent.append(copy)
        return copy

    def fetch(src, dst):
        n = local_count[0]
        local_count[0] += 1
        copy = pltpu.make_async_copy(src, dst, lsem.at[n])
        copy.start()
        return copy

    own_load = fetch(attn, panel.at[0])
    wo_load = {}
    for d in (0, 2, 4, 1, 6, 3, 5, 7):
        first = pl.multiple_of((peer(d) - gr * 8) * feat, feat)
        wo_load[d] = fetch(wo.at[0, pl.ds(first, feat), :], wdb.at[d * feat : (d + 1) * feat])
    res_load = fetch(resid.at[0], resb)
    gain_load = fetch(gain.at[pl.ds(pl.multiple_of(idx % 8 * 8, 8), 8), :], gainb)

    barrier = pltpu.get_barrier_semaphore()
    for mask in (1, 2, 3, 4, 5, 6, 7, 8):
        pl.semaphore_signal(
            barrier, inc=1, device_id={"row": peer(mask)}, device_id_type=pl.DeviceIdType.MESH
        )
    pl.semaphore_wait(barrier, 8)

    gate_up_load = {}

    def load_gate_up(p):
        start, sub = chunks[p]
        for which, (weight, buf) in enumerate(((wg, wgb), (wu, wub))):
            for side, owner in ((1, 1 - core), (0, core)):
                cols = pl.ds(pl.multiple_of(owner * units + start, 256), sub)
                gate_up_load[p, which, side] = fetch(
                    weight.at[0, :, cols], buf.at[side, :, start : start + sub]
                )

    from_x = push(attn, panel.at[XNBR], XNBR)
    from_z = push(attn, panel.at[ZNBR], ZNBR)
    from_core = push(attn, panel.at[CORE], CORE)

    def project(d):
        return jnp.dot(
            panel[d], wdb[d * feat : (d + 1) * feat, :], preferred_element_type=F32
        )

    load_gate_up(0)
    own_load.wait()
    wo_load[0].wait()
    pbuf[...] = project(0)
    from_x.wait_recv()
    mid = toks // 2
    diag_z = push(panel.at[2, 0:mid], panel.at[6, 0:mid], ZNBR)
    core_x = push(panel.at[2], panel.at[3], CORE)
    from_z.wait_recv()
    diag_x = push(panel.at[4, mid:toks], panel.at[6, mid:toks], XNBR)
    core_z = push(panel.at[4], panel.at[5], CORE)
    for d in (1, 2, 4, 3, 5, 6, 7):
        wo_load[d].wait()
    for p in range(1, len(chunks)):
        load_gate_up(p)
    pbuf[...] += project(2)
    pbuf[...] += project(4)
    from_core.wait_recv()
    pbuf[...] += project(1)
    core_x.wait_recv()
    pbuf[...] += project(3)
    diag_z.wait_recv()
    diag_x.wait_recv()
    core_d = push(panel.at[6], panel.at[7], CORE)
    core_z.wait_recv()
    pbuf[...] += project(5)
    pbuf[...] += project(6)
    core_d.wait_recv()
    pbuf[...] += project(7)

    res_load.wait()
    mine = pl.ds(pl.multiple_of(gr * mid, mid), mid)
    pbuf[mine, :] += resb[...].astype(F32)
    from_other = []
    for t in range(BATCHES):
        rows = batch_rows(t)
        psend[rows, :] = pbuf[rows, :].astype(BF)
        if t > 0:
            sent.pop().wait_send()
        from_other.append(push(psend.at[rows], precv.at[rows], OTHER))
    down_load = []
    for start, sub in chunks:
        both = []
        for side, owner in ((0, core), (1, 1 - core)):
            first = pl.multiple_of(owner * units + start, 256)
            to = 2 * start + side * sub
            for part, holder in ((0, gr), (1, 1 - gr)):
                cols = pl.ds(pl.multiple_of(holder * out_w, out_w), out_w)
                both.append(
                    fetch(
                        wd.at[0, pl.ds(first, sub), cols],
                        wdb.at[to : to + sub, part * out_w : (part + 1) * out_w],
                    )
                )
        down_load.append(both)
    gain_load.wait()
    gain_row = jnp.concatenate([gainb[j : j + 1, :] for j in range(8)], axis=1)

    sq_copies = {}

    def receive(t):
        rows = batch_rows(t)
        from_other[t].wait_recv()
        pbuf[rows, :] += precv[rows, :].astype(F32)
        for k in range(4):
            to = slice(t * half + k * blk, t * half + (k + 1) * blk)
            xb[to, :] = (pbuf[token_rows(t, k), :] * gain_row).astype(BF)

    def send_squares(t):
        total = pbuf[batch_rows(t), :]
        total = jnp.sum(total * total, axis=1, keepdims=True)
        total = jnp.broadcast_to(total, (half, toks))
        sq_out[t] = jnp.transpose(jnp.concatenate([total] * BATCHES, axis=0))[0:8, :]
        sq_copies[t] = [
            push(sq_out.at[t], sq_in.at[t, mask - 1], mask) for mask in range(1, 8)
        ]

    def make_scale(t):
        total = sq_out[t]
        for copy in sq_copies[t]:
            copy.wait_recv()
        for k in range(7):
            total = total + sq_in[t, k]
        spread = jnp.transpose(jnp.broadcast_to(total[0:1, :], (toks, toks)))
        scale[batch_rows(t), :] = lax.rsqrt(spread[0:half, :] / D + 1e-05)

    state = {}

    def parts(i):
        span = spans[i]
        quarter = (span.stop - span.start) // 4
        edges = [span.start + n * quarter for n in range(5)]
        return quarter, edges

    def multiply(i):
        t, p = ITEMS[i]
        start, sub = chunks[p]
        quarter, edges = parts(i)
        if i == 0 or ITEMS[i - 1][0] != t:
            receive(t)
        for side in (1, 0):
            for which, weight in enumerate((wgb, wub)):
                if t == 0:
                    gate_up_load[p, which, side].wait()
                value = jnp.dot(
                    xb[batch_rows(t), :],
                    weight[side, :, start : start + sub],
                    preferred_element_type=F32,
                )
                for part in range(2):
                    to = slice(edges[2 * part + which], edges[2 * part + which + 1])
                    at = slice(part * quarter, (part + 1) * quarter)
                    if side:
                        send1[:, to] = value[:, at].astype(BF)
                    else:
                        keep[:, to] = value[:, at]
            if side:
                state["core", i] = push(send1.at[:, spans[i]], recv1.at[:, spans[i]], CORE)
        if i == 0 or ITEMS[i - 1][0] != t:
            send_squares(t)

    def fold_core(i):
        quarter, edges = parts(i)
        a, b = slice(edges[0], edges[2]), slice(edges[2], edges[4])

        def total(first, last, cols):
            rows = slice(first * blk, last * blk)
            return keep[rows, cols] + recv1[rows, cols].astype(F32)

        state["core", i].wait_recv()
        send2[:, a] = total(2, 4, a).astype(BF)
        state["a2", i] = push(send2.at[:, a], recv2.at[:, a], XNBR)
        send2[0:blk, b] = total(1, 2, b).astype(BF)
        send2[blk:two, b] = total(3, 4, b).astype(BF)
        state["b2", i] = push(send2.at[:, b], recv2.at[:, b], ZNBR)
        keep[0:two, a] = total(0, 2, a)
        keep[0:blk, b] = total(0, 1, b)
        keep[two : 3 * blk, b] = total(2, 3, b)

    def fold_second(i):
        quarter, edges = parts(i)
        a, b = slice(edges[0], edges[2]), slice(edges[2], edges[4])
        state["a2", i].wait_recv()
        send3[:, a] = (keep[blk:two, a] + recv2[blk:two, a].astype(F32)).astype(BF)
        state["a3", i] = push(send3.at[:, a], recv3.at[:, a], ZNBR)
        keep[0:blk, a] += recv2[0:blk, a].astype(F32)
        state["b2", i].wait_recv()
        send3[:, b] = (keep[two : 3 * blk, b] + recv2[blk:two, b].astype(F32)).astype(BF)
        state["b3", i] = push(send3.at[:, b], recv3.at[:, b], XNBR)
        keep[0:blk, b] += recv2[0:blk, b].astype(F32)

    def own_units(i):
        quarter, edges = parts(i)
        return slice(edges[0], edges[2]), slice(edges[2], edges[4])

    def activate(i):
        t, p = ITEMS[i]
        quarter, edges = parts(i)
        if i == 0 or ITEMS[i - 1][0] != t:
            make_scale(t)
        factor = scale[token_rows(t, 0), 0:1]
        for part, name in enumerate(("a3", "b3")):
            gates = slice(edges[2 * part], edges[2 * part + 1])
            ups = slice(edges[2 * part + 1], edges[2 * part + 2])
            state[name, i].wait_recv()
            gate = (keep[0:blk, gates] + recv3[:, gates].astype(F32)) * factor
            up = (keep[0:blk, ups] + recv3[:, ups].astype(F32)) * factor
            hidden = gate / (1.0 + jnp.exp(-gate)) * up
            hb[0:blk, edges[part] : edges[part + 1]] = hidden.astype(BF)
        own = own_units(i)[0]
        state["hz", i] = push(hb.at[0:blk, own], hb.at[blk:two, own], ZNBR)
        state["hx", i] = push(hb.at[0:blk, own], hb.at[two : 3 * blk, own], XNBR)

    def relay(i):
        quarter, edges = parts(i)
        own, other = own_units(i)
        first, last = slice(edges[0], edges[1]), slice(edges[1], edges[2])
        far = slice(3 * blk, 4 * blk)
        state["hz", i].wait_recv()
        state["fx", i] = push(hb.at[blk:two, first], hb.at[far, first], XNBR)
        state["hx", i].wait_recv()
        state["fz", i] = push(hb.at[two : 3 * blk, last], hb.at[far, last], ZNBR)
        near = slice(0, 3 * blk)
        state["near", i] = push(hb.at[near, own], hb.at[near, other], CORE)

    def share_last(i):
        own, other = own_units(i)
        far = slice(3 * blk, 4 * blk)
        state["fx", i].wait_recv()
        state["fz", i].wait_recv()
        state["far", i] = push(hb.at[far, own], hb.at[far, other], CORE)

    def down(i):
        t, p = ITEMS[i]
        start, sub = chunks[p]
        opens = i == 0 or ITEMS[i - 1][0] != t
        state["near", i].wait_recv()
        state["far", i].wait_recv()
        if t == 0:
            for load in down_load[p]:
                load.wait()
        rows = slice(2 * start, 2 * start + 2 * sub)
        for part in (1, 0):
            cols = slice(part * out_w, (part + 1) * out_w)
            value = jnp.dot(hb[:, spans[i]], wdb[rows, cols], preferred_element_type=F32)
            if not opens:
                value = acc[batch_rows(t), cols] + value
            if part == 1 and not opens:
                dsend[batch_rows(t), :] = value.astype(BF)
                for k in range(4):
                    at = t * half + k * blk
                    state["down", t, k] = push(
                        dsend.at[at : at + blk], other_out.at[token_rows(t, k)], OTHER
                    )
            else:
                acc[batch_rows(t), cols] = value

    steps = dict(
        m=multiply, f=fold_core, s=fold_second, a=activate, r=relay, l=share_last, d=down
    )
    order = "m0f0m1f1s0m2f2a0s1m3f3r0a1s2l0r1a2d0l1s3r2d1a3l2r3d2l3d3"
    for step, item in zip(order[0::2], order[1::2]):
        steps[step](int(item))

    own_cols = pl.ds(pl.multiple_of(gr * out_w, out_w), out_w)
    for t in range(BATCHES):
        for k in range(4):
            rows = slice(t * half + k * blk, t * half + (k + 1) * blk)
            at = token_rows(t, k)
            own_out[at, :] = pbuf[at, own_cols] + acc[rows, 0:out_w]
    for t in range(BATCHES):
        for k in range(4):
            state["down", t, k].wait_recv()
    for copy in sent:
        copy.wait_send()


def fused(attn_out, residual_in, out_weight, norm_gain, gate_weight, up_weight, down_weight):
    toks, feat = attn_out.shape
    width = out_weight.shape[2]
    ff = gate_weight.shape[2]
    half = toks // BATCHES
    blk = half // 4
    wide = columns_of(ff // 2)[-1].stop
    vm = pltpu.VMEM
    scratch = [
        vm((2, width, ff // 2), BF), vm((2, width, ff // 2), BF), vm((ff, width), BF),
        vm((8, toks, feat), BF), vm((toks // 2, width), BF), vm((8, 128), F32),
        vm((toks, width), F32), vm((toks, width), BF), vm((toks, width), BF),
        vm((toks, width), BF), vm((toks, width), F32),
        vm((BATCHES, 8, toks), F32), vm((BATCHES, 7, 8, toks), F32), vm((toks, toks), F32),
        vm((half, wide), F32), vm((half, wide), BF), vm((half, wide), BF),
        vm((2 * blk, wide), BF), vm((2 * blk, wide), BF),
        vm((blk, wide), BF), vm((blk, wide), BF),
        vm((half, wide), BF), vm((toks, width // 2), BF),
        pltpu.SemaphoreType.DMA((48,)),
        pltpu.SemaphoreType.DMA((96,)), pltpu.SemaphoreType.DMA((96,)),
    ]
    flops = 2 * toks * width * (8 * feat + 3 * ff)
    traffic = 2 * width * (8 * feat + 3 * ff)
    own, other = pl.pallas_call(
        grid_kernel,
        out_shape=(
            jax.ShapeDtypeStruct((toks, width // 2), F32),
            jax.ShapeDtypeStruct((toks, width // 2), BF),
        ),
        in_specs=[pl.BlockSpec(memory_space=pl.ANY)] * 7,
        out_specs=(
            pl.BlockSpec(memory_space=pltpu.VMEM), pl.BlockSpec(memory_space=pl.ANY)
        ),
        scratch_shapes=scratch,
        compiler_params=pltpu.CompilerParams(
            collective_id=0, has_side_effects=True, vmem_limit_bytes=62 * 2**20
        ),
        cost_estimate=pl.CostEstimate(flops=flops, bytes_accessed=traffic, transcendentals=0),
    )(
        attn_out, residual_in, out_weight, norm_gain.reshape(-1, 128),
        gate_weight, up_weight, down_weight,
    )
    return (own + other.astype(F32)).astype(BF)[:, None, :]


def solution(mesh):
    in_specs = (
        P("groups", "row"),
        P("row", "groups", None),
        P("row", None, None),
        P(),
        P("row", None, None),
        P("row", None, None),
        P("row", None, None),
    )
    out_specs = P("groups", "row", None)
    body = fused if mesh.shape["row"] == 2 * COLG else local
    return jax.shard_map(body, mesh=mesh, in_specs=in_specs, out_specs=out_specs, check_vma=False)
```

```python
import jax
import jax.numpy as jnp
from jax import lax
from jax.experimental import pallas as pl
from jax.experimental.pallas import tpu as pltpu
from jax.sharding import PartitionSpec as P

D = 8192
COLG = 8


def from_partner(value, axis, stride):
    mask = 2**stride
    pairs = [(source, source ^ mask) for source in range(lax.axis_size(axis))]
    return lax.ppermute(value, axis, pairs)


def gather_bits(value, dim, bit_list, device_pos, sender):
    for bit_pos in bit_list:
        incoming = sender(value, bit_pos)
        on_low = device_pos >> bit_pos & 1 == 0
        value = jnp.where(
            on_low, jnp.concatenate([value, incoming], dim), jnp.concatenate([incoming, value], dim)
        )
    return value


def reduce_bits(value, dim, bit_list, device_pos, sender):
    for bit_pos in reversed(bit_list):
        middle = value.shape[dim] // 2
        bottom = lax.slice_in_dim(value, 0, middle, axis=dim)
        top_part = lax.slice_in_dim(value, middle, 2 * middle, axis=dim)
        on_low = device_pos >> bit_pos & 1 == 0
        kept = jnp.where(on_low, bottom, top_part)
        outgoing = jnp.where(on_low, top_part, bottom)
        value = kept + sender(outgoing, bit_pos)
    return value


def sum_bits(value, bit_list, sender):
    for bit_pos in bit_list:
        value = value + sender(value, bit_pos)
    return value


def local(attn_out, residual_in, out_weight, norm_gain, gate_weight, up_weight, down_weight):
    all_bits = lax.axis_size("row").bit_length() - 1
    col_count = COLG.bit_length() - 1
    col_bits = list(range(col_count))
    row_bits = list(range(col_count, all_bits))
    device_pos = lax.axis_index("row")
    col_index = device_pos % COLG
    row_index = device_pos // COLG
    panel_in = gather_bits(
        attn_out,
        1,
        col_bits,
        device_pos,
        lambda block_piece, bit_pos: from_partner(block_piece, "row", bit_pos),
    )
    partial_proj = jnp.dot(panel_in, out_weight[0], preferred_element_type=jnp.float32)
    projected = reduce_bits(
        partial_proj,
        0,
        row_bits,
        device_pos,
        lambda block_piece, bit_pos: from_partner(block_piece, "row", bit_pos),
    )
    stream = (residual_in[0].astype(jnp.float32) + projected).astype(jnp.bfloat16)
    widened = stream.astype(jnp.float32)
    feat_cols = widened.shape[1]
    squares = jnp.sum(widened * widened, axis=-1)
    squares = sum_bits(
        squares, col_bits, lambda block_piece, bit_pos: from_partner(block_piece, "row", bit_pos)
    )
    mean_square = (squares / D)[:, None]
    gain_part = lax.dynamic_slice_in_dim(norm_gain, col_index * feat_cols, feat_cols)
    normed = (widened * lax.rsqrt(mean_square + 1e-05) * gain_part).astype(jnp.bfloat16)
    token_rows = gather_bits(
        normed,
        0,
        row_bits,
        device_pos,
        lambda block_piece, bit_pos: from_partner(block_piece, "row", bit_pos),
    )
    gate_vals = jnp.dot(token_rows, gate_weight[0], preferred_element_type=jnp.float32)
    up_vals = jnp.dot(token_rows, up_weight[0], preferred_element_type=jnp.float32)
    stacked = jnp.stack([gate_vals, up_vals])
    summed = reduce_bits(
        stacked,
        1,
        col_bits,
        device_pos,
        lambda block_piece, bit_pos: from_partner(block_piece, "row", bit_pos),
    )
    hidden = (jax.nn.silu(summed[0]) * summed[1]).astype(jnp.bfloat16)
    hidden_rows = gather_bits(
        hidden,
        0,
        col_bits,
        device_pos,
        lambda block_piece, bit_pos: from_partner(block_piece, "row", bit_pos),
    )
    partial_down = jnp.dot(hidden_rows, down_weight[0], preferred_element_type=jnp.float32)
    piece_width = feat_cols // 2 ** len(row_bits)
    stream_rows = gather_bits(
        stream,
        0,
        row_bits,
        device_pos,
        lambda block_piece, bit_pos: from_partner(block_piece, "row", bit_pos),
    )
    stream_piece = lax.dynamic_slice_in_dim(stream_rows, row_index * piece_width, piece_width, 1)
    down_piece = reduce_bits(
        partial_down,
        1,
        row_bits,
        device_pos,
        lambda block_piece, bit_pos: from_partner(block_piece, "row", bit_pos),
    )
    result = (stream_piece.astype(jnp.float32) + down_piece).astype(jnp.bfloat16)
    return result[:, None, :]


BF = jnp.bfloat16
F32 = jnp.float32
CORE, XNBR, ZNBR, OTHER = 1, 2, 4, 8
BATCHES = 2
SHARES = (1, 2, 2, 2)
ITEMS = ((0, 0), (0, 1), (0, 2), (0, 3), (1, 3), (1, 2), (1, 1), (1, 0))
ORDER = (
    "g0m0g1f0m1g2f1s0m2g3f2m3s1a0f3g4s2m4a1r0f4s3g5a2r1l0",
    "m5g6f5s4a3r2d0l1m6f6d1s5a4r3g7l2m7s6f7d2a5r4l3a6s7d3",
    "r5l4r6a7d4l5l6r7d5l7d6d7",
)


def chunks_of(units):
    one = units // sum(SHARES)
    return [(one * sum(SHARES[:p]), one * share) for p, share in enumerate(SHARES)]


def columns_of(units):
    spans, start = [], 0
    for t, p in ITEMS:
        wide = 2 * chunks_of(units)[p][1]
        spans.append(slice(start, start + wide))
        start += wide
    return spans


def grid_kernel(
    attn, resid, wo, gain, wg, wu, wd, own_out, other_out,
    wgb, wub, wdb, panel, resb, gainb, pbuf, psend, precv, xb, acc,
    sq_out, sq_in, scale, keep, send1, recv1, send2, recv2, send3, recv3, hb,
    dsend, lsem, ssem, rsem,
):
    idx = lax.axis_index("row")
    core, xpos, zpos, gr = idx % 2, idx // 2 % 2, idx // 4 % 2, idx // 8
    bits = (core, xpos, zpos, gr)
    toks, width = pbuf.shape
    half = toks // BATCHES
    blk = half // 4
    two = 2 * blk
    feat = panel.shape[2]
    units = wgb.shape[2]
    out_w = width // 2
    chunks = chunks_of(units)
    spans = columns_of(units)

    def peer(mask):
        moved = idx
        for pos, bit in enumerate(bits):
            if mask >> pos & 1:
                moved = moved + (1 - 2 * bit) * 2**pos
        return moved

    own_block = xpos * 2 + zpos
    flip_x, flip_z = 2 * (1 - 2 * xpos), 1 - 2 * zpos
    block_at = (
        own_block, own_block + flip_z, own_block + flip_x, own_block + flip_x + flip_z
    )

    def token_rows(t, k):
        return pl.ds(pl.multiple_of(t * half + block_at[k] * blk, blk), blk)

    def batch_rows(t):
        return slice(t * half, (t + 1) * half)

    count = [0]
    sent = []
    local_count = [0]

    def push(src, dst, mask):
        n = count[0]
        count[0] += 1
        copy = pltpu.make_async_remote_copy(
            src_ref=src, dst_ref=dst, send_sem=ssem.at[n], recv_sem=rsem.at[n],
            device_id={"row": peer(mask)}, device_id_type=pl.DeviceIdType.MESH,
        )
        copy.start()
        sent.append(copy)
        return copy

    def fetch(src, dst):
        n = local_count[0]
        local_count[0] += 1
        copy = pltpu.make_async_copy(src, dst, lsem.at[n])
        copy.start()
        return copy

    own_load = fetch(attn, panel.at[0])
    wo_load = {}
    for d in (0, 2, 4, 1, 6, 3, 5, 7):
        first = pl.multiple_of((peer(d) - gr * 8) * feat, feat)
        wo_load[d] = fetch(wo.at[0, pl.ds(first, feat), :], wdb.at[d * feat : (d + 1) * feat])
    res_load = fetch(resid.at[0], resb)
    gain_load = fetch(gain.at[pl.ds(pl.multiple_of(idx % 8 * 8, 8), 8), :], gainb)

    barrier = pltpu.get_barrier_semaphore()
    for mask in (1, 2, 3, 4, 5, 6, 7, 8):
        pl.semaphore_signal(
            barrier, inc=1, device_id={"row": peer(mask)}, device_id_type=pl.DeviceIdType.MESH
        )
    pl.semaphore_wait(barrier, 8)

    gate_up_load = {}

    def load_gate_up(p):
        start, sub = chunks[p]
        for which, (weight, buf) in enumerate(((wg, wgb), (wu, wub))):
            for side, owner in ((1, 1 - core), (0, core)):
                cols = pl.ds(pl.multiple_of(owner * units + start, 256), sub)
                gate_up_load[p, which, side] = fetch(
                    weight.at[0, :, cols], buf.at[side, :, start : start + sub]
                )

    from_x = push(attn, panel.at[XNBR], XNBR)
    from_z = push(attn, panel.at[ZNBR], ZNBR)
    from_core = push(attn, panel.at[CORE], CORE)

    def project(d):
        return jnp.dot(
            panel[d], wdb[d * feat : (d + 1) * feat, :], preferred_element_type=F32
        )

    own_load.wait()
    wo_load[0].wait()
    pbuf[...] = project(0)
    from_x.wait_recv()
    mid = toks // 2
    diag_z = push(panel.at[2, 0:mid], panel.at[6, 0:mid], ZNBR)
    core_x = push(panel.at[2], panel.at[3], CORE)
    from_z.wait_recv()
    diag_x = push(panel.at[4, mid:toks], panel.at[6, mid:toks], XNBR)
    core_z = push(panel.at[4], panel.at[5], CORE)
    for d in (1, 2, 4, 3, 5, 6, 7):
        wo_load[d].wait()
    for p in (0, 1):
        load_gate_up(p)
    pbuf[...] += project(2)
    pbuf[...] += project(4)
    from_core.wait_recv()
    pbuf[...] += project(1)
    core_x.wait_recv()
    pbuf[...] += project(3)
    diag_z.wait_recv()
    diag_x.wait_recv()
    core_d = push(panel.at[6], panel.at[7], CORE)
    core_z.wait_recv()
    pbuf[...] += project(5)
    pbuf[...] += project(6)
    core_d.wait_recv()
    pbuf[...] += project(7)

    res_load.wait()
    mine = pl.ds(pl.multiple_of(gr * mid, mid), mid)
    pbuf[mine, :] += resb[...].astype(F32)
    from_other = []
    for t in range(BATCHES):
        rows = batch_rows(t)
        psend[rows, :] = pbuf[rows, :].astype(BF)
        if t > 0:
            sent.pop().wait_send()
        from_other.append(push(psend.at[rows], precv.at[rows], OTHER))
    for p in (2, 3):
        load_gate_up(p)
    gain_load.wait()
    gain_row = jnp.concatenate([gainb[j : j + 1, :] for j in range(8)], axis=1)

    sq_copies = {}

    def receive(t):
        rows = batch_rows(t)
        from_other[t].wait_recv()
        pbuf[rows, :] += precv[rows, :].astype(F32)
        for k in range(4):
            to = slice(t * half + k * blk, t * half + (k + 1) * blk)
            xb[to, :] = (pbuf[token_rows(t, k), :] * gain_row).astype(BF)

    def send_squares(t):
        total = pbuf[batch_rows(t), :]
        total = jnp.sum(total * total, axis=1, keepdims=True)
        total = jnp.broadcast_to(total, (half, toks))
        sq_out[t] = jnp.transpose(jnp.concatenate([total] * BATCHES, axis=0))[0:8, :]
        sq_copies[t] = [
            push(sq_out.at[t], sq_in.at[t, mask - 1], mask) for mask in range(1, 8)
        ]

    def make_scale(t):
        total = sq_out[t]
        for copy in sq_copies[t]:
            copy.wait_recv()
        for k in range(7):
            total = total + sq_in[t, k]
        spread = jnp.transpose(jnp.broadcast_to(total[0:1, :], (toks, toks)))
        scale[batch_rows(t), :] = lax.rsqrt(spread[0:half, :] / D + 1e-05)

    state = {}
    down_load = []

    def load_down():
        for start, sub in chunks:
            both = []
            for side, owner in ((0, core), (1, 1 - core)):
                first = pl.multiple_of(owner * units + start, 256)
                to = 2 * start + side * sub
                for part, holder in ((0, gr), (1, 1 - gr)):
                    cols = pl.ds(pl.multiple_of(holder * out_w, out_w), out_w)
                    both.append(
                        fetch(
                            wd.at[0, pl.ds(first, sub), cols],
                            wdb.at[to : to + sub, part * out_w : (part + 1) * out_w],
                        )
                    )
            down_load.append(both)


    def parts(i):
        span = spans[i]
        quarter = (span.stop - span.start) // 4
        edges = [span.start + n * quarter for n in range(5)]
        return quarter, edges

    def opens(i):
        return i == 0 or ITEMS[i - 1][0] != ITEMS[i][0]

    def product(i, side):
        t, p = ITEMS[i]
        start, sub = chunks[p]
        quarter, edges = parts(i)
        for which, weight in enumerate((wgb, wub)):
            if t == 0:
                gate_up_load[p, which, side].wait()
            value = jnp.dot(
                xb[batch_rows(t), :],
                weight[side, :, start : start + sub],
                preferred_element_type=F32,
            )
            for part in range(2):
                to = slice(edges[2 * part + which], edges[2 * part + which + 1])
                at = slice(part * quarter, (part + 1) * quarter)
                if side:
                    send1[:, to] = value[:, at].astype(BF)
                else:
                    keep[:, to] = value[:, at]

    def give(i):
        if opens(i):
            receive(ITEMS[i][0])
        product(i, 1)
        state["core", i] = push(send1.at[:, spans[i]], recv1.at[:, spans[i]], CORE)

    def multiply(i):
        product(i, 0)
        if opens(i):
            send_squares(ITEMS[i][0])

    def fold_core(i):
        quarter, edges = parts(i)
        a, b = slice(edges[0], edges[2]), slice(edges[2], edges[4])

        def total(first, last, cols):
            rows = slice(first * blk, last * blk)
            return keep[rows, cols] + recv1[rows, cols].astype(F32)

        state["core", i].wait_recv()
        send2[:, a] = total(2, 4, a).astype(BF)
        state["a2", i] = push(send2.at[:, a], recv2.at[:, a], XNBR)
        send2[0:blk, b] = total(1, 2, b).astype(BF)
        send2[blk:two, b] = total(3, 4, b).astype(BF)
        state["b2", i] = push(send2.at[:, b], recv2.at[:, b], ZNBR)
        keep[0:two, a] = total(0, 2, a)
        keep[0:blk, b] = total(0, 1, b)
        keep[two : 3 * blk, b] = total(2, 3, b)

    def fold_second(i):
        quarter, edges = parts(i)
        a, b = slice(edges[0], edges[2]), slice(edges[2], edges[4])
        state["a2", i].wait_recv()
        send3[:, a] = (keep[blk:two, a] + recv2[blk:two, a].astype(F32)).astype(BF)
        state["a3", i] = push(send3.at[:, a], recv3.at[:, a], ZNBR)
        keep[0:blk, a] += recv2[0:blk, a].astype(F32)
        state["b2", i].wait_recv()
        send3[:, b] = (keep[two : 3 * blk, b] + recv2[blk:two, b].astype(F32)).astype(BF)
        state["b3", i] = push(send3.at[:, b], recv3.at[:, b], XNBR)
        keep[0:blk, b] += recv2[0:blk, b].astype(F32)

    def own_units(i):
        quarter, edges = parts(i)
        return slice(edges[0], edges[2]), slice(edges[2], edges[4])

    def activate(i):
        t, p = ITEMS[i]
        quarter, edges = parts(i)
        if opens(i):
            make_scale(t)
        factor = scale[token_rows(t, 0), 0:1]
        for part, name in enumerate(("a3", "b3")):
            gates = slice(edges[2 * part], edges[2 * part + 1])
            ups = slice(edges[2 * part + 1], edges[2 * part + 2])
            state[name, i].wait_recv()
            gate = (keep[0:blk, gates] + recv3[:, gates].astype(F32)) * factor
            up = (keep[0:blk, ups] + recv3[:, ups].astype(F32)) * factor
            hidden = gate / (1.0 + jnp.exp(-gate)) * up
            hb[0:blk, edges[part] : edges[part + 1]] = hidden.astype(BF)
        own = own_units(i)[0]
        state["hz", i] = push(hb.at[0:blk, own], hb.at[blk:two, own], ZNBR)
        state["hx", i] = push(hb.at[0:blk, own], hb.at[two : 3 * blk, own], XNBR)

    def relay(i):
        quarter, edges = parts(i)
        own, other = own_units(i)
        first, last = slice(edges[0], edges[1]), slice(edges[1], edges[2])
        far = slice(3 * blk, 4 * blk)
        state["hz", i].wait_recv()
        state["fx", i] = push(hb.at[blk:two, first], hb.at[far, first], XNBR)
        state["hx", i].wait_recv()
        state["fz", i] = push(hb.at[two : 3 * blk, last], hb.at[far, last], ZNBR)
        near = slice(0, 3 * blk)
        state["near", i] = push(hb.at[near, own], hb.at[near, other], CORE)

    def share_last(i):
        own, other = own_units(i)
        far = slice(3 * blk, 4 * blk)
        state["fx", i].wait_recv()
        state["fz", i].wait_recv()
        state["far", i] = push(hb.at[far, own], hb.at[far, other], CORE)

    def down(i):
        t, p = ITEMS[i]
        start, sub = chunks[p]
        closes = i + 1 == len(ITEMS) or opens(i + 1)
        state["near", i].wait_recv()
        state["far", i].wait_recv()
        if t == 0:
            for load in down_load[p]:
                load.wait()
        rows = slice(2 * start, 2 * start + 2 * sub)
        for part in (1, 0):
            cols = slice(part * out_w, (part + 1) * out_w)
            value = jnp.dot(hb[:, spans[i]], wdb[rows, cols], preferred_element_type=F32)
            if not opens(i):
                value = acc[batch_rows(t), cols] + value
            if part == 1 and closes:
                dsend[batch_rows(t), :] = value.astype(BF)
                for k in range(4):
                    at = t * half + k * blk
                    state["down", t, k] = push(
                        dsend.at[at : at + blk], other_out.at[token_rows(t, k)], OTHER
                    )
            else:
                acc[batch_rows(t), cols] = value

    steps = dict(
        g=give, m=multiply, f=fold_core, s=fold_second,
        a=activate, r=relay, l=share_last, d=down,
    )
    for line in ORDER:
        for step, item in zip(line[0::2], line[1::2]):
            steps[step](int(item))
            if step + item == "m1":
                load_down()

    own_cols = pl.ds(pl.multiple_of(gr * out_w, out_w), out_w)
    for t in range(BATCHES):
        for k in range(4):
            rows = slice(t * half + k * blk, t * half + (k + 1) * blk)
            at = token_rows(t, k)
            own_out[at, :] = pbuf[at, own_cols] + acc[rows, 0:out_w]
    for t in range(BATCHES):
        for k in range(4):
            state["down", t, k].wait_recv()
    for copy in sent:
        copy.wait_send()


def fused(attn_out, residual_in, out_weight, norm_gain, gate_weight, up_weight, down_weight):
    toks, feat = attn_out.shape
    width = out_weight.shape[2]
    ff = gate_weight.shape[2]
    half = toks // BATCHES
    blk = half // 4
    wide = columns_of(ff // 2)[-1].stop
    vm = pltpu.VMEM
    scratch = [
        vm((2, width, ff // 2), BF), vm((2, width, ff // 2), BF), vm((ff, width), BF),
        vm((8, toks, feat), BF), vm((toks // 2, width), BF), vm((8, 128), F32),
        vm((toks, width), F32), vm((toks, width), BF), vm((toks, width), BF),
        vm((toks, width), BF), vm((toks, width), F32),
        vm((BATCHES, 8, toks), F32), vm((BATCHES, 7, 8, toks), F32), vm((toks, toks), F32),
        vm((half, wide), F32), vm((half, wide), BF), vm((half, wide), BF),
        vm((2 * blk, wide), BF), vm((2 * blk, wide), BF),
        vm((blk, wide), BF), vm((blk, wide), BF),
        vm((half, wide), BF), vm((toks, width // 2), BF),
        pltpu.SemaphoreType.DMA((48,)),
        pltpu.SemaphoreType.DMA((128,)), pltpu.SemaphoreType.DMA((128,)),
    ]
    flops = 2 * toks * width * (8 * feat + 3 * ff)
    traffic = 2 * width * (8 * feat + 3 * ff)
    own, other = pl.pallas_call(
        grid_kernel,
        out_shape=(
            jax.ShapeDtypeStruct((toks, width // 2), F32),
            jax.ShapeDtypeStruct((toks, width // 2), BF),
        ),
        in_specs=[pl.BlockSpec(memory_space=pl.ANY)] * 7,
        out_specs=(
            pl.BlockSpec(memory_space=pltpu.VMEM), pl.BlockSpec(memory_space=pl.ANY)
        ),
        scratch_shapes=scratch,
        compiler_params=pltpu.CompilerParams(
            collective_id=0, has_side_effects=True, vmem_limit_bytes=62 * 2**20
        ),
        cost_estimate=pl.CostEstimate(flops=flops, bytes_accessed=traffic, transcendentals=0),
    )(
        attn_out, residual_in, out_weight, norm_gain.reshape(-1, 128),
        gate_weight, up_weight, down_weight,
    )
    return (own + other.astype(F32)).astype(BF)[:, None, :]


def solution(mesh):
    in_specs = (
        P("groups", "row"),
        P("row", "groups", None),
        P("row", None, None),
        P(),
        P("row", None, None),
        P("row", None, None),
        P("row", None, None),
    )
    out_specs = P("groups", "row", None)
    body = fused if mesh.shape["row"] == 2 * COLG else local
    return jax.shard_map(body, mesh=mesh, in_specs=in_specs, out_specs=out_specs, check_vma=False)
```
